256 devices in a mesh: seq: 32 (over y, x, core), ch: 8 (over z).
Axes of the slice: x: 4, y: 4, z: 8, core: 2. Of those that a mesh axis runs over, the one named last changes fastest.
Arguments:
- gate_query: bfloat16 [16384, 4096], P('seq', 'ch'), may hold values from -6 to 6
- gate_key: bfloat16 [16384, 4096], P('seq', 'ch'), may hold values from -6 to 6
- gate_value: bfloat16 [16384, 4096], P('seq', 'ch'), may hold values from -6 to 6
- skip_gain: float32 [4096], P('ch'), may hold values from 0.5 to 1.5
- filter_spectra: bfloat16 [32768, 2, 4096], P('seq', None, 'ch'), may hold values from -9 to 9
- out_weight: bfloat16 [4096, 4096], P('ch'), may hold values from -0.09375 to 0.09375
Outputs:
- mixed: bfloat16 [16384, 4096], P('seq', 'ch')
The draws below stay inside these ranges and needn't reach their ends.
All inputs are finite; a program needn't handle non-finite values.
Results may differ from the reference program's by a relative error of at most 0.0049.
Values may be sent and summed in bfloat16 or wider, within the bound.
A program may use at most 128 MiB of HBM per device.

```python
import jax
import jax.numpy as jnp

CH = 4096
DOUT = 4096
TOKENS = 16384
NFREQ = 32768


def block_levels(own_key, shape, cuts, smallest, largest):
    gain, own = 1.0, jax.random.fold_in(own_key, 6)
    for axis_at, blocks in cuts:
        draws = jnp.exp(jax.random.uniform(jax.random.fold_in(own, axis_at), (blocks,), jnp.float32, smallest / len(cuts), largest / len(cuts)))
        gain = gain * jnp.repeat(draws, shape[axis_at] // blocks).reshape([-1 if axis == axis_at else 1 for axis in range(len(shape))])
    return gain


def scatter_about(own_key, shape, scale, bound, cuts=(), held_as=jnp.bfloat16):
    gain = block_levels(own_key, shape, cuts, -0.22, 0.18) if cuts else 1.0
    values = jax.random.normal(own_key, shape, jnp.float32) * scale * gain
    return jnp.minimum(jnp.maximum(values, -bound), bound).astype(held_as)


def setup_inputs(seed: int = 0) -> dict:
    splits = jax.random.split(jax.random.key(seed), 7)
    gate_query = scatter_about(splits[0], (TOKENS, CH), 1.0, 6.0, ((0, 32), (1, 8)))
    gate_key = scatter_about(splits[1], (TOKENS, CH), 1.0, 6.0, ((0, 32), (1, 8)))
    gate_value = scatter_about(splits[2], (TOKENS, CH), 1.0, 6.0, ((0, 32), (1, 8)))
    skip_gain = jnp.clip(0.5 + 1.0 * jax.random.uniform(splits[3], (CH,), jnp.float32) ** block_levels(splits[3], (CH,), ((0, 8),), -0.2, 0.2), 0.5, 1.5)
    filter_spectra = scatter_about(splits[4], (NFREQ, 2, CH), 1.5, 9.0, ((0, 32), (2, 8)))
    out_weight = scatter_about(splits[5], (CH, DOUT), CH ** -0.5, 0.09375, ((0, 8),))
    return dict(gate_query=gate_query, gate_key=gate_key, gate_value=gate_value, skip_gain=skip_gain, filter_spectra=filter_spectra, out_weight=out_weight)


def reference(gate_query, gate_key, gate_value, skip_gain, filter_spectra, out_weight):
    gated_in = gate_key.astype(jnp.float32) * gate_value.astype(jnp.float32)
    length = gated_in.shape[0]
    channels = gated_in.shape[1]
    stride = 512 if channels % 512 == 0 else channels
    pieces = []
    for offset in range(0, channels, stride):
        columns = gated_in[:, offset:offset + stride]
        spectrum = jnp.fft.fft(columns, n=2 * length, axis=0)
        real_part = filter_spectra[:, 0, offset:offset + stride].astype(jnp.float32)
        imag_part = filter_spectra[:, 1, offset:offset + stride].astype(jnp.float32)
        response = real_part + 1j * imag_part
        pieces.append(jnp.real(jnp.fft.ifft(spectrum * response, axis=0))[:length])
    convolved = jnp.concatenate(pieces, axis=1)
    mixed_in = (gate_query.astype(jnp.float32) * (convolved + skip_gain[None, :] * gated_in)).astype(jnp.bfloat16)
    return jnp.dot(mixed_in, out_weight, preferred_element_type=jnp.float32).astype(jnp.bfloat16)
```

```python
import functools

import jax
import jax.numpy as jnp
import ml_dtypes
import numpy as np
from jax import lax
from jax.experimental import pallas as pl
from jax.experimental.pallas import tpu as pltpu
from jax.sharding import PartitionSpec as P

S = 32
C = 16
T = 512
R = 64
K = 512
LANES = 128
KL = 16
N = R * K
VMEM = pltpu.VMEM


def halves(table):
    table = np.asarray(table, np.float64)
    high = table.astype(ml_dtypes.bfloat16)
    low = (table - high.astype(np.float64)).astype(ml_dtypes.bfloat16)
    return high, low


@functools.lru_cache(None)
def tables():
    p, s = np.arange(R), np.arange(S)
    tau, kappa = np.arange(T), np.arange(K)
    cross = 2 * np.pi * np.outer(p, s) / R
    first = np.concatenate([np.cos(cross), -np.sin(cross)], 0)
    first = np.concatenate(halves(first), 1)
    turn = 2 * np.pi * np.outer(p, tau) / N
    inner = 2 * np.pi * (np.outer(kappa, tau) % K) / K
    inner = np.concatenate([np.cos(inner), np.sin(inner)], 1)
    inner_high, inner_low = halves(inner)
    last = np.concatenate([np.cos(cross).T, -np.sin(cross).T], 1) / N
    last_high, last_low = halves(last)
    last = np.concatenate([last_high, last_low, last_high], 1)
    order = np.zeros((2 * R, 2 * R), ml_dtypes.bfloat16)
    for q in range(R):
        for part in range(2):
            order[2 * q + part, part * R + q] = 1
    return dict(
        first=first,
        turn_cos=np.cos(turn).astype(np.float32),
        turn_sin=np.sin(turn).astype(np.float32),
        inner_high=inner_high,
        inner_low=inner_low,
        last=last,
        order=order,
    )


def dot(left, right, left_dim, right_dim):
    return lax.dot_general(
        left, right, (((left_dim,), (right_dim,)), ((), ())), preferred_element_type=jnp.float32
    )


def split(values):
    high = values.astype(jnp.bfloat16)
    return high, (values - high.astype(jnp.float32)).astype(jnp.bfloat16)


def prepare_kernel(key_ref, value_ref, spectra_ref, order_ref, gated_ref, filter_ref, wide):
    gated = key_ref[...].astype(jnp.float32) * value_ref[...].astype(jnp.float32)
    gated_ref[...] = gated.T.astype(jnp.bfloat16)

    @pl.loop(0, KL)
    def _(k):
        block = spectra_ref[pl.ds(pl.multiple_of(k * 2 * R, 2 * R), 2 * R), :]
        wide[pl.ds(k, T, stride=KL), :] = dot(block, order_ref[...], 0, 0)

    @pl.loop(0, T // C)
    def _(i):
        rows = pl.ds(pl.multiple_of(i * C * KL, C * KL), C * KL)
        filter_ref[rows, :] = wide[rows, :].astype(jnp.bfloat16)


def convolve_channel(gated, response, first, turn_cos, turn_sin, inner_high, inner_low, last):
    upper = dot(first, jnp.concatenate([gated, gated], 0), 1, 0)
    real, imag = upper[:R], upper[R:]
    turned_real = real * turn_cos + imag * turn_sin
    turned_imag = imag * turn_cos - real * turn_sin
    real_high, real_low = split(turned_real)
    imag_high, imag_low = split(turned_imag)
    high = jnp.concatenate(
        [jnp.concatenate([real_high, imag_high], 1), jnp.concatenate([imag_high, -real_high], 1)], 0
    )
    low = jnp.concatenate(
        [jnp.concatenate([real_low, imag_low], 1), jnp.concatenate([imag_low, -real_low], 1)], 0
    )
    spectrum = dot(inner_high, high, 1, 1) + (dot(inner_high, low, 1, 1) + dot(inner_low, high, 1, 1))
    lane = lax.broadcasted_iota(jnp.int32, (K, 2 * R), 1)
    is_real = lane < R
    swapped = pltpu.roll(response, R, 1)
    both_real = jnp.where(is_real, response, swapped)
    both_imag = jnp.where(is_real, -swapped, response)
    product = spectrum * both_real + pltpu.roll(spectrum, R, 1) * both_imag
    product_high, product_low = split(product)
    back = dot(product_high, inner_high, 0, 0) + (
        dot(product_low, inner_high, 0, 0) + dot(product_high, inner_low, 0, 0)
    )
    back_real = back[:R, :T] - back[R:, T:]
    back_imag = back[:R, T:] + back[R:, :T]
    out_real = back_real * turn_cos - back_imag * turn_sin
    out_imag = back_real * turn_sin + back_imag * turn_cos
    out_high, out_low = split(jnp.concatenate([out_real, out_imag], 0))
    return dot(last, jnp.concatenate([out_high, out_high, out_low], 0), 1, 0)


def convolve_kernel(
    gated_ref, filter_ref, first, turn_cos, turn_sin, inner_high, inner_low, last, out_ref, wide, result
):
    for i in range(T // LANES):
        lanes = slice(i * LANES, (i + 1) * LANES)
        wide[i] = gated_ref[:, :, lanes].reshape(S * C, LANES).astype(jnp.float32)

    @pl.loop(0, C)
    def _(c):
        rows = pl.ds(c, S, stride=C)
        gated = jnp.concatenate([wide[i, rows, :] for i in range(T // LANES)], 1)
        response = filter_ref[:, c].reshape(K, 2 * R).astype(jnp.float32)
        convolved = convolve_channel(
            gated.astype(jnp.bfloat16),
            response,
            first[...],
            turn_cos[...],
            turn_sin[...],
            inner_high[...],
            inner_low[...],
            last[...],
        )
        for i in range(T // LANES):
            result[i, rows, :] = convolved[:, i * LANES : (i + 1) * LANES]

    for i in range(T // LANES):
        lanes = slice(i * LANES, (i + 1) * LANES)
        out_ref[:, :, lanes] = result[i].astype(jnp.bfloat16).reshape(S, C, LANES)


def combine_kernel(conv_ref, query_ref, key_ref, value_ref, gain_ref, mixed_ref):
    gated = key_ref[...].astype(jnp.float32) * value_ref[...].astype(jnp.float32)
    convolved = conv_ref[...].astype(jnp.float32).T
    mixed = query_ref[...].astype(jnp.float32) * (convolved + gain_ref[...] * gated)
    mixed_ref[...] = mixed.astype(jnp.bfloat16)


def whole(count):
    return [pl.BlockSpec(memory_space=VMEM)] * count


def body(gate_query, gate_key, gate_value, skip_gain, filter_spectra, out_weight):
    tab = {name: jnp.asarray(table) for name, table in tables().items()}
    groups = lax.axis_size("ch")
    rank = lax.axis_index("seq")
    outputs = out_weight.shape[1] // groups
    params = pltpu.CompilerParams(vmem_limit_bytes=48 << 20)

    share = lax.dynamic_slice_in_dim(out_weight, rank * C, C, 0)
    share = lax.all_to_all(
        share.reshape(C, groups, outputs), "ch", split_axis=1, concat_axis=0, tiled=False
    )
    weight = lax.all_gather(share.reshape(groups, C, outputs), "seq", axis=0)
    weight = jnp.transpose(weight, (1, 0, 2, 3)).reshape(groups * T, outputs)

    gated, response = pl.pallas_call(
        prepare_kernel,
        out_shape=(
            jax.ShapeDtypeStruct((T, T), jnp.bfloat16),
            jax.ShapeDtypeStruct((T * KL, 2 * R), jnp.bfloat16),
        ),
        in_specs=whole(4),
        out_specs=tuple(whole(2)),
        scratch_shapes=[VMEM((T * KL, 2 * R), jnp.float32)],
        compiler_params=params,
    )(gate_key, gate_value, filter_spectra.reshape(KL * R * 2, T), tab["order"])
    gated = lax.all_to_all(gated.reshape(S, C, T), "seq", split_axis=0, concat_axis=0, tiled=True)
    response = lax.all_to_all(
        response.reshape(S, C, KL, 2 * R), "seq", split_axis=0, concat_axis=0, tiled=True
    )
    names = ("first", "turn_cos", "turn_sin", "inner_high", "inner_low", "last")
    convolved = pl.pallas_call(
        convolve_kernel,
        out_shape=jax.ShapeDtypeStruct((S, C, T), jnp.bfloat16),
        in_specs=whole(8),
        out_specs=whole(1)[0],
        scratch_shapes=[VMEM((T // LANES, S * C, LANES), jnp.float32)] * 2,
        compiler_params=params,
    )(gated, response, *(tab[name] for name in names))
    convolved = lax.all_to_all(convolved, "seq", split_axis=0, concat_axis=0, tiled=True)
    mixed = pl.pallas_call(
        combine_kernel,
        out_shape=jax.ShapeDtypeStruct((T, T), jnp.bfloat16),
        in_specs=whole(5),
        out_specs=whole(1)[0],
        compiler_params=params,
    )(convolved.reshape(S * C, T), gate_query, gate_key, gate_value, skip_gain[None, :])
    mixed = lax.all_gather(mixed, "ch", axis=1, tiled=True)
    return jnp.dot(mixed, weight, preferred_element_type=jnp.float32).astype(jnp.bfloat16)


def solution(mesh):
    placed = (
        P("seq", "ch"),
        P("seq", "ch"),
        P("seq", "ch"),
        P("ch"),
        P("seq", None, "ch"),
        P("ch", None),
    )
    return jax.shard_map(
        body, mesh=mesh, in_specs=placed, out_specs=P("seq", "ch"), check_vma=False
    )
```

```python
import functools

import jax
import jax.numpy as jnp
import ml_dtypes
import numpy as np
from jax import lax
from jax.experimental import pallas as pl
from jax.experimental.pallas import tpu as pltpu
from jax.sharding import PartitionSpec as P

S = 32
C = 16
Q = 4
G = C // Q
T = 512
R = 64
K = 512
L = 128
KL = K // S
N = R * K
MESH = pl.DeviceIdType.MESH
VMEM = pltpu.VMEM
BF16, F32 = jnp.bfloat16, jnp.float32


def halves(table):
    table = np.asarray(table, np.float64)
    high = table.astype(ml_dtypes.bfloat16)
    low = (table - high.astype(np.float64)).astype(ml_dtypes.bfloat16)
    return high, low


@functools.lru_cache(None)
def tables():
    p, s = np.arange(R), np.arange(S)
    tau, kappa = np.arange(T), np.arange(K)
    cross = 2 * np.pi * np.outer(p, s) / R
    each = np.eye(Q)
    first = np.concatenate([np.cos(cross), -np.sin(cross)], 0)
    first = np.concatenate(halves(np.kron(each, first)), 1)
    turn = 2 * np.pi * np.outer(p, tau) / N
    inner = 2 * np.pi * (np.outer(kappa, tau) % K) / K
    inner = np.concatenate([np.cos(inner), np.sin(inner)], 1)
    inner_high, inner_low = halves(inner)
    last = np.concatenate([np.cos(cross).T, -np.sin(cross).T], 1) / N
    last_high, last_low = halves(np.kron(each, last))
    last = np.concatenate([last_high, last_low, last_high], 1)
    order = np.zeros((2 * R, 2 * R), ml_dtypes.bfloat16)
    for q in range(R):
        for part in range(2):
            order[2 * q + part, part * R + q] = 1
    spread = np.zeros((T, T), ml_dtypes.bfloat16)
    gather = np.zeros((T, T), ml_dtypes.bfloat16)
    for j in range(S):
        for g in range(G):
            for c in range(Q):
                spread[j * C + g * Q + c, g * L + j * Q + c] = 1
                gather[(g * Q + c) * S + j, j * C + g * Q + c] = 1
    return dict(
        first=first,
        turn_cos=np.cos(turn).astype(np.float32),
        turn_sin=np.sin(turn).astype(np.float32),
        inner_high=inner_high,
        inner_low=inner_low,
        last=last,
        order=order,
        spread=spread,
        gather=gather,
    )


NAMES = (
    "first", "turn_cos", "turn_sin", "inner_high", "inner_low", "last", "order", "spread", "gather"
)


def dot(left, right, left_dim, right_dim):
    return lax.dot_general(
        left, right, (((left_dim,), (right_dim,)), ((), ())), preferred_element_type=F32
    )


def split(values):
    high = values.astype(BF16)
    return high, (values - high.astype(F32)).astype(BF16)


def chunk_lanes(g):
    return pl.ds(pl.multiple_of(g * L, L), L)


def seq_kernel(
    query, key, value, gain, spectra, first, turn_cos, turn_sin, inner_high, inner_low, last,
    order, spread, gather, mixed, gated_out, gated_in, filter_out, filter_in, conv_out, conv_in,
    wide, sorted_in, rows, spectrum, product, back, turned, staging, sent_gated, sent_filter,
    sent_conv, got_gated, got_filter, got_conv,
):
    me = lax.axis_index("seq")

    def peer(k):
        return lax.rem(me + k, S)

    barrier = pltpu.get_barrier_semaphore()

    @pl.loop(1, S)
    def _(k):
        pl.semaphore_signal(barrier, inc=1, device_id={"seq": peer(k)}, device_id_type=MESH)

    def send_all(source, target, sent, sem):
        @pl.loop(1, S)
        def _(k):
            pltpu.make_async_remote_copy(
                src_ref=source.at[peer(k)],
                dst_ref=target.at[me],
                send_sem=sent,
                recv_sem=sem,
                device_id={"seq": peer(k)},
                device_id_type=MESH,
            ).start()

        target[me] = source[me]

    def arrive(target, sem):
        most = target.at[pl.ds(0, S - 1)]
        pltpu.make_async_copy(most, most, sem).wait()

    def gated_values():
        return key[...].astype(F32) * value[...].astype(F32)

    def prepare_filter(g):
        @pl.loop(0, KL)
        def _(k):
            block = spectra[pl.ds(pl.multiple_of(k * 2 * R, 2 * R), 2 * R), chunk_lanes(g)]
            wide[pl.ds(k, L, stride=KL), :] = dot(block, order[...], 0, 0)

        filter_out[g] = wide[...].astype(BF16).reshape(S, Q, KL, L)

    gated_out[...] = (
        dot(spread[...], gated_values().astype(BF16), 1, 1).astype(BF16).reshape(S, C, T)
    )
    pl.semaphore_wait(barrier, S - 1)
    send_all(gated_out, gated_in, sent_gated, got_gated)

    @pl.loop(0, G)
    def _(g):
        prepare_filter(g)
        send_all(filter_out.at[g], filter_in.at[g], sent_filter.at[g], got_filter.at[g])

    arrive(gated_in, got_gated)
    sorted_in[...] = dot(gather[...], gated_in[...].reshape(T, T), 1, 0).astype(BF16)

    @pl.loop(0, G)
    def _(g):
        values = sorted_in[pl.ds(pl.multiple_of(g * L, L), L), :]
        back[:, :T] = dot(first[...], jnp.concatenate([values, values], 0), 1, 0)
        for c in range(Q):
            at = c * 2 * R
            real, imag = back[at : at + R, :T], back[at + R : at + 2 * R, :T]
            turned_real = (real * turn_cos[...] + imag * turn_sin[...]).astype(BF16)
            turned_imag = (imag * turn_cos[...] - real * turn_sin[...]).astype(BF16)
            rows[at : at + R, :T] = turned_real
            rows[at : at + R, T:] = turned_imag
            rows[at + R : at + 2 * R, :T] = turned_imag
            rows[at + R : at + 2 * R, T:] = -turned_real
        spectrum[g] = dot(inner_high[...], rows[...], 1, 1) + dot(inner_low[...], rows[...], 1, 1)

    def convolve(g):
        arrive(filter_in.at[g], got_filter.at[g])
        is_real = lax.broadcasted_iota(jnp.int32, (K, L), 1) < R
        for c in range(Q):
            lanes = slice(c * L, (c + 1) * L)
            response = filter_in[g, :, c].reshape(K, L).astype(F32)
            swapped = pltpu.roll(response, R, 1)
            value_c = spectrum[g, :, lanes]
            product[:, lanes] = (
                value_c * jnp.where(is_real, response, swapped)
                + pltpu.roll(value_c, R, 1) * jnp.where(is_real, -swapped, response)
            ).astype(BF16)
        back[...] = dot(product[...], inner_high[...], 0, 0) + dot(product[...], inner_low[...], 0, 0)
        for c in range(Q):
            at = c * 2 * R
            real = back[at : at + R, :T] - back[at + R : at + 2 * R, T:]
            imag = back[at : at + R, T:] + back[at + R : at + 2 * R, :T]
            for at, part in (
                (at, real * turn_cos[...] - imag * turn_sin[...]),
                (at + R, real * turn_sin[...] + imag * turn_cos[...]),
            ):
                high, low = split(part)
                turned[at : at + R, :] = high
                turned[T + at : T + at + R, :] = high
                turned[2 * T + at : 2 * T + at + R, :] = low
        result = dot(last[...], turned[...], 1, 0)
        for c in range(Q):
            for i in range(T // L):
                staging[pl.ds(c * Q + i, S, stride=C), :] = result[
                    c * S : (c + 1) * S, i * L : (i + 1) * L
                ]
        conv_out[g] = staging[...].astype(BF16).reshape(S, C, L)
        send_all(conv_out.at[g], conv_in.at[g], sent_conv.at[g], got_conv.at[g])

    def combine(g):
        arrive(conv_in.at[g], got_conv.at[g])
        staging[...] = conv_in[g].reshape(T, L).astype(F32)
        lanes = chunk_lanes(g)
        for i in range(T // L):
            tokens = slice(i * L, (i + 1) * L)
            convolved = staging[pl.ds(i, L, stride=Q), :].T
            gated = key[tokens, lanes].astype(F32) * value[tokens, lanes].astype(F32)
            mixed[tokens, lanes] = (
                query[tokens, lanes].astype(F32) * (convolved + gain[:, lanes] * gated)
            ).astype(BF16)

    convolve(0)

    @pl.loop(1, G)
    def _(g):
        convolve(g)
        combine(g - 1)

    combine(G - 1)
    arrive(gated_out, sent_gated)
    for g in range(G):
        arrive(filter_out.at[g], sent_filter.at[g])
        arrive(conv_out.at[g], sent_conv.at[g])


def whole(count):
    return [pl.BlockSpec(memory_space=VMEM)] * count


def body(gate_query, gate_key, gate_value, skip_gain, filter_spectra, out_weight):
    tab = tables()
    groups = lax.axis_size("ch")
    rank = lax.axis_index("seq")
    outputs = out_weight.shape[1] // groups

    share = lax.dynamic_slice_in_dim(out_weight, rank * C, C, 0)
    share = lax.all_to_all(
        share.reshape(C, groups, outputs), "ch", split_axis=1, concat_axis=0, tiled=False
    )
    weight = lax.all_gather(share.reshape(groups, C, outputs), "seq", axis=0)
    weight = jnp.transpose(weight, (1, 0, 2, 3)).reshape(groups * T, outputs)

    dma = pltpu.SemaphoreType.DMA
    mixed = pl.pallas_call(
        seq_kernel,
        out_shape=jax.ShapeDtypeStruct((T, T), BF16),
        in_specs=whole(5 + len(NAMES)),
        out_specs=whole(1)[0],
        scratch_shapes=[
            VMEM((S, C, T), BF16),
            VMEM((S, C, T), BF16),
            VMEM((G, S, Q, KL, L), BF16),
            VMEM((G, S, Q, KL, L), BF16),
            VMEM((G, S, C, L), BF16),
            VMEM((G, S, C, L), BF16),
            VMEM((L * KL, L), F32),
            VMEM((T, T), BF16),
            VMEM((T, 2 * T), BF16),
            VMEM((G, K, T), F32),
            VMEM((K, T), BF16),
            VMEM((T, 2 * T), F32),
            VMEM((3 * T, T), BF16),
            VMEM((T, L), F32),
            dma(()),
            dma((G,)),
            dma((G,)),
            dma(()),
            dma((G,)),
            dma((G,)),
        ],
        compiler_params=pltpu.CompilerParams(
            collective_id=0, has_side_effects=True, vmem_limit_bytes=52 << 20
        ),
        cost_estimate=pl.CostEstimate(flops=12 * 10**9, bytes_accessed=8 << 20, transcendentals=0),
    )(
        gate_query,
        gate_key,
        gate_value,
        skip_gain[None, :],
        filter_spectra.reshape(KL * R * 2, T),
        *(jnp.asarray(tab[name]) for name in NAMES),
    )
    mixed = lax.all_gather(mixed, "ch", axis=1, tiled=True)
    return jnp.dot(mixed, weight, preferred_element_type=F32).astype(BF16)


def solution(mesh):
    placed = (
        P("seq", "ch"),
        P("seq", "ch"),
        P("seq", "ch"),
        P("ch"),
        P("seq", None, "ch"),
        P("ch", None),
    )
    return jax.shard_map(
        body, mesh=mesh, in_specs=placed, out_specs=P("seq", "ch"), check_vma=False
    )
```

```python
import functools

import jax
import jax.numpy as jnp
import ml_dtypes
import numpy as np
from jax import lax
from jax.experimental import pallas as pl
from jax.experimental.pallas import tpu as pltpu
from jax.sharding import PartitionSpec as P

S = 32
Z = 8
C = 16
Q = 4
G = C // Q
T = 512
R = 64
K = 512
L = 128
KL = K // S
N = R * K
MESH = pl.DeviceIdType.MESH
VMEM = pltpu.VMEM
BF16, F32 = jnp.bfloat16, jnp.float32


def halves(table):
    table = np.asarray(table, np.float64)
    high = table.astype(ml_dtypes.bfloat16)
    low = (table - high.astype(np.float64)).astype(ml_dtypes.bfloat16)
    return high, low


@functools.lru_cache(None)
def tables():
    p, s = np.arange(R), np.arange(S)
    tau, kappa = np.arange(T), np.arange(K)
    cross = 2 * np.pi * np.outer(p, s) / R
    each = np.eye(Q)
    first = np.concatenate([np.cos(cross), -np.sin(cross)], 0)
    first = np.concatenate(halves(np.kron(each, first)), 1)
    turn = 2 * np.pi * np.outer(p, tau) / N
    inner = 2 * np.pi * (np.outer(kappa, tau) % K) / K
    inner = np.concatenate([np.cos(inner), np.sin(inner)], 1)
    inner_high, inner_low = halves(inner)
    last = np.concatenate([np.cos(cross).T, -np.sin(cross).T], 1) / N
    last_high, last_low = halves(np.kron(each, last))
    last = np.concatenate([last_high, last_low, last_high], 1)
    order = np.zeros((2 * R * G, 2 * R * G), ml_dtypes.bfloat16)
    for q in range(R):
        for g in range(G):
            for part in range(2):
                order[(q * G + g) * 2 + part, (g * 2 + part) * R + q] = 1
    spread = np.zeros((T, T), ml_dtypes.bfloat16)
    gather = np.zeros((T, T), ml_dtypes.bfloat16)
    for j in range(S):
        for g in range(G):
            for c in range(Q):
                spread[j * C + g * Q + c, g * L + j * Q + c] = 1
                gather[(g * Q + c) * S + j, j * C + g * Q + c] = 1
    return dict(
        first=first,
        turn_cos=np.cos(turn).astype(np.float32),
        turn_sin=np.sin(turn).astype(np.float32),
        inner_high=inner_high,
        inner_low=inner_low,
        last=last,
        order=order,
        spread=spread,
        gather=gather,
    )


NAMES = (
    "first", "turn_cos", "turn_sin", "inner_high", "inner_low", "last", "order", "spread", "gather"
)


def dot(left, right, left_dim, right_dim):
    return lax.dot_general(
        left, right, (((left_dim,), (right_dim,)), ((), ())), preferred_element_type=F32
    )


def split(values):
    high = values.astype(BF16)
    return high, (values - high.astype(F32)).astype(BF16)


def chunk_lanes(g):
    return pl.ds(pl.multiple_of(g * L, L), L)


def kernel(
    query, key, value, gain, spectra, weight_here, first, turn_cos, turn_sin, inner_high, inner_low,
    last, order, spread, gather, out, gated_out, gated_in, filter_out, filter_in, conv_out, conv_in,
    share, weight, mixed, wide, sorted_in, rows, spectrum, product, back, turned, staging, local,
    sent_gated, sent_filter, sent_conv, sent_share, sent_weight, sent_ring, got_gated, got_filter,
    got_conv, got_share, got_weight, got_ring,
):
    me, level = lax.axis_index("seq"), lax.axis_index("ch")
    core, x, y = lax.rem(me, 2), lax.rem(me // 2, 4), me // 8
    sibling = me + 1 - 2 * core

    def peer(k):
        return lax.rem(me + k, S)

    def at_level(k):
        return lax.rem(level + k + Z, Z)

    def along_x(k):
        return y * 8 + lax.rem(x + k, 4) * 2 + core

    def along_y(k):
        return lax.rem(y + k, 4) * 8 + x * 2 + core

    share_load = pltpu.make_async_copy(
        weight_here.at[pl.ds(pl.multiple_of(me * C, C), C), :], share, local
    )
    share_load.start()
    barrier = pltpu.get_barrier_semaphore()

    @pl.loop(1, S)
    def _(k):
        pl.semaphore_signal(barrier, inc=1, device_id={"seq": peer(k)}, device_id_type=MESH)

    @pl.loop(1, Z)
    def _(k):
        pl.semaphore_signal(barrier, inc=1, device_id={"ch": at_level(k)}, device_id_type=MESH)

    def send(source, target, sent, got, **to):
        pltpu.make_async_remote_copy(
            src_ref=source, dst_ref=target, send_sem=sent, recv_sem=got, device_id=to,
            device_id_type=MESH,
        ).start()

    def send_all(source, target, sent, got):
        @pl.loop(1, S)
        def _(k):
            send(source.at[peer(k)], target.at[me], sent, got, seq=peer(k))

        target[me] = source[me]

    def wait(ref, sem):
        pltpu.make_async_copy(ref, ref, sem).wait()

    def arrive(target, sem):
        wait(target.at[pl.ds(0, S - 1)], sem)

    def share_lanes(k):
        return pl.ds(pl.multiple_of(k * T, T), T)

    def spread_share():
        @pl.loop(1, Z)
        def _(k):
            to = at_level(k)
            send(
                share.at[:, share_lanes(to)], weight.at[level, me], sent_share, got_share, ch=to
            )

        weight[level, me] = share[:, share_lanes(level)]

    lower, upper = pl.ds(0, Z // 2), pl.ds(Z // 2, Z // 2)

    def weight_first():
        wait(weight.at[pl.ds(0, Z - 1), 0], got_share)

        @pl.loop(1, 4)
        def _(k):
            part = weight.at[lower, me]
            send(part, part, sent_weight.at[0], got_weight.at[0], seq=along_x(k))
            part = weight.at[upper, me]
            send(part, part, sent_weight.at[1], got_weight.at[1], seq=along_y(k))

    def weight_second():
        wait(weight.at[lower, pl.ds(0, 3)], got_weight.at[0])
        wait(weight.at[upper, pl.ds(0, 3)], got_weight.at[1])

        @pl.loop(1, 4)
        def _(k):
            @pl.loop(0, 4)
            def _(i):
                part = weight.at[lower, along_x(i)]
                send(part, part, sent_weight.at[2], got_weight.at[2], seq=along_y(k))
                part = weight.at[upper, along_y(i)]
                send(part, part, sent_weight.at[3], got_weight.at[3], seq=along_x(k))

    def weight_third():
        wait(weight.at[lower, pl.ds(0, 12)], got_weight.at[2])
        wait(weight.at[upper, pl.ds(0, 12)], got_weight.at[3])

        @pl.loop(0, S // 2)
        def _(i):
            part = weight.at[:, 2 * i + core]
            send(part, part, sent_weight.at[4], got_weight.at[4], seq=sibling)

    def weight_sent():
        wait(weight.at[pl.ds(0, Z - 1), 0], sent_share)
        wait(weight.at[lower, pl.ds(0, 3)], sent_weight.at[0])
        wait(weight.at[upper, pl.ds(0, 3)], sent_weight.at[1])
        wait(weight.at[lower, pl.ds(0, 12)], sent_weight.at[2])
        wait(weight.at[upper, pl.ds(0, 12)], sent_weight.at[3])
        wait(weight.at[:, pl.ds(0, S // 2)], sent_weight.at[4])

    def ring_part(way, hop, g, source):
        tokens = pl.ds(0, T)
        if hop == Z // 2:
            tokens = pl.ds(way * (T // 2), T // 2)
        return mixed.at[source, tokens, chunk_lanes(g)]

    def ring_send(hop, g):
        for way, sign in enumerate((1, -1)):
            part = ring_part(way, hop, g, at_level(-sign * (hop - 1)))
            send(
                part, part, sent_ring.at[way, hop - 1, g], got_ring.at[way, hop - 1, g],
                ch=at_level(sign),
            )

    def ring_arrive(hop, g):
        for way, sign in enumerate((1, -1)):
            wait(ring_part(way, hop, g, at_level(-sign * hop)), got_ring.at[way, hop - 1, g])

    def forward(hop, g):
        ring_arrive(hop - 1, g)
        ring_send(hop, g)

    def gated_values():
        return key[...].astype(F32) * value[...].astype(F32)

    def prepare_filter():
        @pl.loop(0, KL)
        def _(k):
            block = spectra[pl.ds(pl.multiple_of(k * T, T), T), :]
            moved = dot(block, order[...], 0, 0)
            for g in range(G):
                wide[g, pl.ds(k, L, stride=KL), :] = moved[:, g * L : (g + 1) * L]

    gated_out[...] = (
        dot(spread[...], gated_values().astype(BF16), 1, 1).astype(BF16).reshape(S, C, T)
    )
    pl.semaphore_wait(barrier, S + Z - 2)
    send_all(gated_out, gated_in, sent_gated, got_gated)
    share_load.wait()
    spread_share()
    prepare_filter()

    @pl.loop(0, G)
    def _(g):
        filter_out[g] = wide[g].astype(BF16).reshape(S, Q, KL, L)
        send_all(filter_out.at[g], filter_in.at[g], sent_filter.at[g], got_filter.at[g])

    weight_first()
    arrive(gated_in, got_gated)
    sorted_in[...] = dot(gather[...], gated_in[...].reshape(T, T), 1, 0).astype(BF16)

    @pl.loop(0, G)
    def _(g):
        values = sorted_in[pl.ds(pl.multiple_of(g * L, L), L), :]
        back[:, :T] = dot(first[...], jnp.concatenate([values, values], 0), 1, 0)
        for c in range(Q):
            at = c * 2 * R
            real, imag = back[at : at + R, :T], back[at + R : at + 2 * R, :T]
            turned_real = (real * turn_cos[...] + imag * turn_sin[...]).astype(BF16)
            turned_imag = (imag * turn_cos[...] - real * turn_sin[...]).astype(BF16)
            rows[at : at + R, :T] = turned_real
            rows[at : at + R, T:] = turned_imag
            rows[at + R : at + 2 * R, :T] = turned_imag
            rows[at + R : at + 2 * R, T:] = -turned_real
        spectrum[g] = dot(inner_high[...], rows[...], 1, 1) + dot(inner_low[...], rows[...], 1, 1)

    def convolve(g):
        arrive(filter_in.at[g], got_filter.at[g])
        is_real = lax.broadcasted_iota(jnp.int32, (K, L), 1) < R
        for c in range(Q):
            lanes = slice(c * L, (c + 1) * L)
            response = filter_in[g, :, c].reshape(K, L).astype(F32)
            swapped = pltpu.roll(response, R, 1)
            value_c = spectrum[g, :, lanes]
            product[:, lanes] = (
                value_c * jnp.where(is_real, response, swapped)
                + pltpu.roll(value_c, R, 1) * jnp.where(is_real, -swapped, response)
            ).astype(BF16)
        back[...] = dot(product[...], inner_high[...], 0, 0) + dot(product[...], inner_low[...], 0, 0)
        for c in range(Q):
            at = c * 2 * R
            real = back[at : at + R, :T] - back[at + R : at + 2 * R, T:]
            imag = back[at : at + R, T:] + back[at + R : at + 2 * R, :T]
            for at, part in (
                (at, real * turn_cos[...] - imag * turn_sin[...]),
                (at + R, real * turn_sin[...] + imag * turn_cos[...]),
            ):
                high, low = split(part)
                turned[at : at + R, :] = high
                turned[T + at : T + at + R, :] = high
                turned[2 * T + at : 2 * T + at + R, :] = low
        result = dot(last[...], turned[...], 1, 0)
        for c in range(Q):
            for i in range(T // L):
                staging[pl.ds(c * Q + i, S, stride=C), :] = result[
                    c * S : (c + 1) * S, i * L : (i + 1) * L
                ]
        conv_out[g] = staging[...].astype(BF16).reshape(S, C, L)
        send_all(conv_out.at[g], conv_in.at[g], sent_conv.at[g], got_conv.at[g])

    def combine(g):
        arrive(conv_in.at[g], got_conv.at[g])
        staging[...] = conv_in[g].reshape(T, L).astype(F32)
        lanes = chunk_lanes(g)
        for i in range(T // L):
            tokens = slice(i * L, (i + 1) * L)
            convolved = staging[pl.ds(i, L, stride=Q), :].T
            gated = key[tokens, lanes].astype(F32) * value[tokens, lanes].astype(F32)
            mixed[level, tokens, lanes] = (
                query[tokens, lanes].astype(F32) * (convolved + gain[:, lanes] * gated)
            ).astype(BF16)
        ring_send(1, g)

    convolve(0)

    @pl.loop(1, G)
    def _(g):
        convolve(g)

        @pl.when(g >= 2)
        def _():
            forward(2, g - 2)

        combine(g - 1)

        @pl.when(g >= 2)
        def _():
            forward(3, g - 2)

        @pl.when(g >= 3)
        def _():
            forward(4, g - 3)

    weight_second()
    combine(G - 1)
    forward(2, G - 2)
    forward(4, G - 3)
    forward(2, G - 1)
    forward(3, G - 2)
    weight_third()
    forward(3, G - 1)
    forward(4, G - 2)
    forward(4, G - 1)
    for g in range(G):
        ring_arrive(Z // 2, g)
    wait(weight.at[:, pl.ds(0, S // 2)], got_weight.at[4])

    total = spectrum.at[0]
    total[...] = jnp.zeros((T, T), F32)

    @pl.loop(0, Z)
    def _(z):
        total[...] += dot(mixed[z], weight[z].reshape(T, T), 1, 0)

    out[...] = total[...].astype(BF16)
    arrive(gated_out, sent_gated)
    weight_sent()
    for g in range(G):
        arrive(filter_out.at[g], sent_filter.at[g])
        arrive(conv_out.at[g], sent_conv.at[g])
        for hop in range(1, Z // 2 + 1):
            for way in range(2):
                wait(ring_part(way, hop, g, 0), sent_ring.at[way, hop - 1, g])


def whole(count):
    return [pl.BlockSpec(memory_space=VMEM)] * count


def body(gate_query, gate_key, gate_value, skip_gain, filter_spectra, out_weight):
    tab = tables()
    spectra = filter_spectra.reshape(KL * R, 2, G, L).transpose(0, 2, 1, 3)
    dma = pltpu.SemaphoreType.DMA
    return pl.pallas_call(
        kernel,
        out_shape=jax.ShapeDtypeStruct((T, T), BF16),
        in_specs=whole(5) + [pl.BlockSpec(memory_space=pl.ANY)] + whole(len(NAMES)),
        out_specs=whole(1)[0],
        scratch_shapes=[
            VMEM((S, C, T), BF16),
            VMEM((S, C, T), BF16),
            VMEM((G, S, Q, KL, L), BF16),
            VMEM((G, S, Q, KL, L), BF16),
            VMEM((G, S, C, L), BF16),
            VMEM((G, S, C, L), BF16),
            VMEM((C, Z * T), BF16),
            VMEM((Z, S, C, T), BF16),
            VMEM((Z, T, T), BF16),
            VMEM((G, L * KL, L), F32),
            VMEM((T, T), BF16),
            VMEM((T, 2 * T), BF16),
            VMEM((G, K, T), F32),
            VMEM((K, T), BF16),
            VMEM((T, 2 * T), F32),
            VMEM((3 * T, T), BF16),
            VMEM((T, L), F32),
            dma(()),
            dma(()),
            dma((G,)),
            dma((G,)),
            dma(()),
            dma((5,)),
            dma((2, Z // 2, G)),
            dma(()),
            dma((G,)),
            dma((G,)),
            dma(()),
            dma((5,)),
            dma((2, Z // 2, G)),
        ],
        compiler_params=pltpu.CompilerParams(
            collective_id=0, has_side_effects=True, vmem_limit_bytes=52 << 20
        ),
        cost_estimate=pl.CostEstimate(flops=12 * 10**9, bytes_accessed=8 << 20, transcendentals=0),
    )(
        gate_query,
        gate_key,
        gate_value,
        skip_gain[None, :],
        spectra.reshape(KL * R * G * 2, L),
        out_weight,
        *(jnp.asarray(tab[name]) for name in NAMES),
    )


def solution(mesh):
    placed = (
        P("seq", "ch"),
        P("seq", "ch"),
        P("seq", "ch"),
        P("ch"),
        P("seq", None, "ch"),
        P("ch", None),
    )
    return jax.shard_map(
        body, mesh=mesh, in_specs=placed, out_specs=P("seq", "ch"), check_vma=False
    )
```

```python
import functools

import jax
import jax.numpy as jnp
import ml_dtypes
import numpy as np
from jax import lax
from jax.experimental import pallas as pl
from jax.experimental.pallas import tpu as pltpu
from jax.sharding import PartitionSpec as P

S = 32
Z = 8
C = 16
Q = 4
G = C // Q
T = 512
R = 64
K = 512
L = 128
KL = K // S
N = R * K
MESH = pl.DeviceIdType.MESH
VMEM = pltpu.VMEM
BF16, F32 = jnp.bfloat16, jnp.float32


def halves(table):
    table = np.asarray(table, np.float64)
    high = table.astype(ml_dtypes.bfloat16)
    low = (table - high.astype(np.float64)).astype(ml_dtypes.bfloat16)
    return high, low


@functools.lru_cache(None)
def tables():
    p, s = np.arange(R), np.arange(S)
    tau, kappa = np.arange(T), np.arange(K)
    cross = 2 * np.pi * np.outer(p, s) / R
    each = np.eye(Q)
    first = np.concatenate([np.cos(cross), -np.sin(cross)], 0)
    first = np.concatenate(halves(np.kron(each, first)), 1)
    turn = 2 * np.pi * np.outer(p, tau) / N
    inner = 2 * np.pi * (np.outer(kappa, tau) % K) / K
    inner = np.concatenate([np.cos(inner), np.sin(inner)], 1)
    inner_high, inner_low = halves(inner)
    last = np.concatenate([np.cos(cross).T, -np.sin(cross).T], 1) / N
    last_high, last_low = halves(np.kron(each, last))
    last = np.concatenate([last_high, last_low, last_high], 1)
    order = np.zeros((2 * R * G, 2 * R * G), ml_dtypes.bfloat16)
    for q in range(R):
        for g in range(G):
            for part in range(2):
                order[(q * G + g) * 2 + part, (g * 2 + part) * R + q] = 1
    return dict(
        order=order,
        first=first,
        turn=np.concatenate([np.cos(turn), np.sin(turn)], 0).astype(np.float32),
        inner=np.stack([inner_high, inner_low]),
        last=last,
    )


NAMES = ("order", "first", "turn", "inner", "last")


def dot(left, right, left_dim, right_dim):
    return lax.dot_general(
        left, right, (((left_dim,), (right_dim,)), ((), ())), preferred_element_type=F32
    )


def split(values):
    high = values.astype(BF16)
    return high, (values - high.astype(F32)).astype(BF16)


def chunk_lanes(g):
    return pl.ds(pl.multiple_of(g * L, L), L)


def kernel(
    query_here, key_here, value_here, gain_here, spectra_here, weight_here, order_here, first_here,
    turn_here, inner_here, last_here, out, query, key, value, gain, spectra, order, first, turn,
    inner, last, gated_out, gated_in, filter_out, filter_in, conv_out, conv_in, share, weight, mixed,
    wide, rows, spectrum, product, back, turned, staging, loaded, sent_gated, sent_filter, sent_conv,
    sent_share, sent_weight, sent_ring, got_gated, got_filter, got_conv, got_share, got_weight,
    got_ring,
):
    me, level = lax.axis_index("seq"), lax.axis_index("ch")
    core, x, y = lax.rem(me, 2), lax.rem(me // 2, 4), me // 8
    sibling = me + 1 - 2 * core

    def peer(k):
        away_x = lax.rem(k, 4)
        away_y = lax.rem(k // 4 + away_x, 4)
        return (
            lax.rem(y + away_y, 4) * 8 + lax.rem(x + away_x, 4) * 2 + lax.rem(core + k // 16, 2)
        )

    def at_level(k):
        return lax.rem(level + k + Z, Z)

    def along_x(k):
        return y * 8 + lax.rem(x + k, 4) * 2 + core

    def along_y(k):
        return lax.rem(y + k, 4) * 8 + x * 2 + core

    barrier = pltpu.get_barrier_semaphore()

    @pl.loop(1, S)
    def _(k):
        pl.semaphore_signal(barrier, inc=1, device_id={"seq": peer(k)}, device_id_type=MESH)

    @pl.loop(1, Z)
    def _(k):
        pl.semaphore_signal(barrier, inc=1, device_id={"ch": at_level(k)}, device_id_type=MESH)

    share_here = weight_here.at[pl.ds(pl.multiple_of(me * C, C), C), :]
    loads = [
        pltpu.make_async_copy(source, target, loaded.at[i])
        for i, (source, target) in enumerate(
            (
                (key_here, key), (value_here, value), (spectra_here, spectra), (order_here, order),
                (share_here, share), (first_here, first), (turn_here, turn), (inner_here, inner),
                (last_here, last), (query_here, query), (gain_here, gain),
            )
        )
    ]
    for load in loads:
        load.start()

    def send(source, target, sent, got, **to):
        pltpu.make_async_remote_copy(
            src_ref=source, dst_ref=target, send_sem=sent, recv_sem=got, device_id=to,
            device_id_type=MESH,
        ).start()

    def send_all(source, target, sent, got):
        @pl.loop(1, S)
        def _(k):
            send(source.at[peer(k)], target.at[me], sent, got, seq=peer(k))

        target[me] = source[me]

    def wait(ref, sem):
        pltpu.make_async_copy(ref, ref, sem).wait()

    def arrive(target, sem):
        wait(target.at[pl.ds(0, S - 1)], sem)

    def share_lanes(k):
        return pl.ds(pl.multiple_of(k * T, T), T)

    def spread_share():
        @pl.loop(1, Z)
        def _(k):
            to = at_level(k)
            send(
                share.at[:, share_lanes(to)], weight.at[level, me], sent_share, got_share, ch=to
            )

        weight[level, me] = share[:, share_lanes(level)]

    lower, upper = pl.ds(0, Z // 2), pl.ds(Z // 2, Z // 2)

    def weight_first():
        wait(weight.at[pl.ds(0, Z - 1), 0], got_share)

        @pl.loop(1, 4)
        def _(k):
            part = weight.at[lower, me]
            send(part, part, sent_weight.at[0], got_weight.at[0], seq=along_x(k))
            part = weight.at[upper, me]
            send(part, part, sent_weight.at[1], got_weight.at[1], seq=along_y(k))

    def weight_second():
        wait(weight.at[lower, pl.ds(0, 3)], got_weight.at[0])
        wait(weight.at[upper, pl.ds(0, 3)], got_weight.at[1])

        @pl.loop(1, 4)
        def _(k):
            @pl.loop(0, 4)
            def _(i):
                part = weight.at[lower, along_x(i)]
                send(part, part, sent_weight.at[2], got_weight.at[2], seq=along_y(k))
                part = weight.at[upper, along_y(i)]
                send(part, part, sent_weight.at[3], got_weight.at[3], seq=along_x(k))

    def weight_third():
        wait(weight.at[lower, pl.ds(0, 12)], got_weight.at[2])
        wait(weight.at[upper, pl.ds(0, 12)], got_weight.at[3])

        @pl.loop(0, S // 2)
        def _(i):
            part = weight.at[:, 2 * i + core]
            send(part, part, sent_weight.at[4], got_weight.at[4], seq=sibling)

    def weight_sent():
        wait(weight.at[pl.ds(0, Z - 1), 0], sent_share)
        wait(weight.at[lower, pl.ds(0, 3)], sent_weight.at[0])
        wait(weight.at[upper, pl.ds(0, 3)], sent_weight.at[1])
        wait(weight.at[lower, pl.ds(0, 12)], sent_weight.at[2])
        wait(weight.at[upper, pl.ds(0, 12)], sent_weight.at[3])
        wait(weight.at[:, pl.ds(0, S // 2)], sent_weight.at[4])

    def ring_part(way, hop, g, source):
        tokens = pl.ds(0, T)
        if hop == Z // 2:
            tokens = pl.ds(way * (T // 2), T // 2)
        lanes = pl.ds(pl.multiple_of(source * T + g * L, L), L)
        return mixed.at[tokens, lanes]

    def ring_send(hop, g):
        for way, sign in enumerate((1, -1)):
            part = ring_part(way, hop, g, at_level(-sign * (hop - 1)))
            send(
                part, part, sent_ring.at[way, hop - 1, g], got_ring.at[way, hop - 1, g],
                ch=at_level(sign),
            )

    def ring_arrive(hop, g):
        for way, sign in enumerate((1, -1)):
            wait(ring_part(way, hop, g, at_level(-sign * hop)), got_ring.at[way, hop - 1, g])

    def forward(hop, g):
        ring_arrive(hop - 1, g)
        ring_send(hop, g)

    def prepare_gated(g):
        lanes = chunk_lanes(g)
        gated = (key[:, lanes].astype(F32) * value[:, lanes].astype(F32)).T
        for i in range(T // L):
            staging[pl.ds(i, L, stride=Q), :] = gated[:, i * L : (i + 1) * L]
        gated_out[g] = staging[...].astype(BF16).reshape(S, C, L)

    def prepare_filter():
        @pl.loop(0, KL)
        def _(k):
            block = spectra[pl.ds(pl.multiple_of(k * T, T), T), :]
            moved = dot(block, order[...], 0, 0)
            for g in range(G):
                wide[g, pl.ds(k, L, stride=KL), :] = moved[:, g * L : (g + 1) * L]

    def round_filter(g):
        for h in range(2):
            part = wide[g].astype(BF16).reshape(S, Q, KL, L)[:, h * Q // 2 : (h + 1) * Q // 2]
            filter_out[g, h] = part

    def transform(g):
        staging[...] = gated_in[g].reshape(T, L).astype(F32)
        for c in range(Q):
            for i in range(T // L):
                part = staging[pl.ds(c * Q + i, S, stride=C), :].astype(BF16)
                for copy in range(2):
                    at = copy * L + c * S
                    turned[at : at + S, i * L : (i + 1) * L] = part
        back[:, :T] = dot(first[...], turned[: 2 * L, :], 1, 0)
        for c in range(Q):
            at = c * 2 * R
            real, imag = back[at : at + R, :T], back[at + R : at + 2 * R, :T]
            turned_real = (real * turn[:R] + imag * turn[R:]).astype(BF16)
            turned_imag = (imag * turn[:R] - real * turn[R:]).astype(BF16)
            rows[at : at + R, :T] = turned_real
            rows[at : at + R, T:] = turned_imag
            rows[at + R : at + 2 * R, :T] = turned_imag
            rows[at + R : at + 2 * R, T:] = -turned_real
        spectrum[g] = dot(inner[0], rows[...], 1, 1) + dot(inner[1], rows[...], 1, 1)

    def multiply(g):
        is_real = lax.broadcasted_iota(jnp.int32, (K, L), 1) < R
        for c in range(Q):
            lanes = slice(c * L, (c + 1) * L)
            response = filter_in[g, c // 2, :, c % 2].reshape(K, L).astype(F32)
            swapped = pltpu.roll(response, R, 1)
            value_c = spectrum[g, :, lanes]
            product[:, lanes] = (
                value_c * jnp.where(is_real, response, swapped)
                + pltpu.roll(value_c, R, 1) * jnp.where(is_real, -swapped, response)
            ).astype(BF16)

    def invert():
        back[...] = dot(product[...], inner[0], 0, 0) + dot(product[...], inner[1], 0, 0)

    def unturn():
        for c in range(Q):
            at = c * 2 * R
            real = back[at : at + R, :T] - back[at + R : at + 2 * R, T:]
            imag = back[at : at + R, T:] + back[at + R : at + 2 * R, :T]
            for at, part in (
                (at, real * turn[:R] - imag * turn[R:]),
                (at + R, real * turn[R:] + imag * turn[:R]),
            ):
                high, low = split(part)
                turned[at : at + R, :] = high
                turned[T + at : T + at + R, :] = high
                turned[2 * T + at : 2 * T + at + R, :] = low

    def finish(g):
        result = dot(last[...], turned[...], 1, 0)
        for c in range(Q):
            for i in range(T // L):
                staging[pl.ds(c * Q + i, S, stride=C), :] = result[
                    c * S : (c + 1) * S, i * L : (i + 1) * L
                ]
        conv_out[g] = staging[...].astype(BF16).reshape(S, C, L)

    def mix(g):
        staging[...] = conv_in[g].reshape(T, L).astype(F32)
        lanes = chunk_lanes(g)
        for i in range(T // L):
            tokens = slice(i * L, (i + 1) * L)
            convolved = staging[pl.ds(i, L, stride=Q), :].T
            gated = key[tokens, lanes].astype(F32) * value[tokens, lanes].astype(F32)
            mixed[tokens, pl.ds(pl.multiple_of(level * T + g * L, L), L)] = (
                query[tokens, lanes].astype(F32) * (convolved + gain[:, lanes] * gated)
            ).astype(BF16)

    def project():
        out[...] = dot(mixed[...], weight[...].reshape(Z * T, T), 1, 0).astype(BF16)

    def send_gated(g):
        send_all(gated_out.at[g], gated_in.at[g], sent_gated.at[g], got_gated.at[g])

    def send_filter(g, h):
        send_all(
            filter_out.at[g, h], filter_in.at[g, h], sent_filter.at[g, h], got_filter.at[g, h]
        )

    def convolve(g):
        arrive(filter_in.at[g, 0], got_filter.at[g, 0])
        arrive(filter_in.at[g, 1], got_filter.at[g, 1])
        multiply(g)
        invert()
        unturn()
        finish(g)
        send_all(conv_out.at[g], conv_in.at[g], sent_conv.at[g], got_conv.at[g])

    def combine(g):
        arrive(conv_in.at[g], got_conv.at[g])
        mix(g)
        ring_send(1, g)

    for load in loads[:2]:
        load.wait()

    @pl.loop(0, G)
    def _(g):
        prepare_gated(g)

    for load in loads[2:4]:
        load.wait()
    prepare_filter()

    @pl.loop(0, G)
    def _(g):
        round_filter(g)

    for load in loads[4:]:
        load.wait()
    pl.semaphore_wait(barrier, S + Z - 2)
    send_gated(0)
    send_filter(0, 0)
    send_filter(0, 1)
    send_gated(1)
    send_filter(1, 0)
    spread_share()

    @pl.loop(0, G)
    def _(g):
        arrive(gated_in.at[g], got_gated.at[g])
        transform(g)

        @pl.when(g >= 1)
        def _():
            forward(2, g - 1)

        convolve(g)

        @pl.when(g < G - 1)
        def _():
            send_filter(g + 1, 1)

        @pl.when(g < G - 2)
        def _():
            send_gated(g + 2)
            send_filter(g + 2, 0)

        @pl.when(g == 1)
        def _():
            weight_first()

        @pl.when(g == G - 1)
        def _():
            weight_second()

        @pl.when(g >= 1)
        def _():
            forward(3, g - 1)

        combine(g)

        @pl.when(g >= 1)
        def _():
            forward(4, g - 1)

    forward(2, G - 1)
    forward(3, G - 1)
    weight_third()
    forward(4, G - 1)
    for g in range(G):
        ring_arrive(Z // 2, g)
    wait(weight.at[:, pl.ds(0, S // 2)], got_weight.at[4])
    project()
    weight_sent()
    for g in range(G):
        arrive(gated_out.at[g], sent_gated.at[g])
        arrive(filter_out.at[g, 0], sent_filter.at[g, 0])
        arrive(filter_out.at[g, 1], sent_filter.at[g, 1])
        arrive(conv_out.at[g], sent_conv.at[g])
        for hop in range(1, Z // 2 + 1):
            for way in range(2):
                wait(ring_part(way, hop, g, 0), sent_ring.at[way, hop - 1, g])


def body(gate_query, gate_key, gate_value, skip_gain, filter_spectra, out_weight):
    tab = tables()
    spectra = filter_spectra.reshape(KL * R, 2, G, L).transpose(0, 2, 1, 3)
    dma = pltpu.SemaphoreType.DMA
    return pl.pallas_call(
        kernel,
        out_shape=jax.ShapeDtypeStruct((T, T), BF16),
        in_specs=[pl.BlockSpec(memory_space=pltpu.HBM)] * (6 + len(NAMES)),
        out_specs=pl.BlockSpec(memory_space=VMEM),
        scratch_shapes=[
            VMEM((T, T), BF16),
            VMEM((T, T), BF16),
            VMEM((T, T), BF16),
            VMEM((1, T), F32),
            VMEM((KL * R * G * 2, L), BF16),
            VMEM((2 * R * G, 2 * R * G), BF16),
            VMEM((T, 2 * L), BF16),
            VMEM((2 * R, T), F32),
            VMEM((2, K, 2 * T), BF16),
            VMEM((L, 3 * T), BF16),
            VMEM((G, S, C, L), BF16),
            VMEM((G, S, C, L), BF16),
            VMEM((G, 2, S, Q // 2, KL, L), BF16),
            VMEM((G, 2, S, Q // 2, KL, L), BF16),
            VMEM((G, S, C, L), BF16),
            VMEM((G, S, C, L), BF16),
            VMEM((C, Z * T), BF16),
            VMEM((Z, S, C, T), BF16),
            VMEM((T, Z * T), BF16),
            VMEM((G, L * KL, L), F32),
            VMEM((T, 2 * T), BF16),
            VMEM((G, K, T), F32),
            VMEM((K, T), BF16),
            VMEM((T, 2 * T), F32),
            VMEM((3 * T, T), BF16),
            VMEM((T, L), F32),
            dma((11,)),
            dma((G,)),
            dma((G, 2)),
            dma((G,)),
            dma(()),
            dma((5,)),
            dma((2, Z // 2, G)),
            dma((G,)),
            dma((G, 2)),
            dma((G,)),
            dma(()),
            dma((5,)),
            dma((2, Z // 2, G)),
        ],
        compiler_params=pltpu.CompilerParams(
            collective_id=0, has_side_effects=True, vmem_limit_bytes=58 << 20
        ),
        cost_estimate=pl.CostEstimate(flops=12 * 10**9, bytes_accessed=8 << 20, transcendentals=0),
    )(
        gate_query,
        gate_key,
        gate_value,
        skip_gain[None, :],
        spectra.reshape(KL * R * G * 2, L),
        out_weight,
        *(jnp.asarray(tab[name]) for name in NAMES),
    )


def solution(mesh):
    placed = (
        P("seq", "ch"),
        P("seq", "ch"),
        P("seq", "ch"),
        P("ch"),
        P("seq", None, "ch"),
        P("ch", None),
    )
    return jax.shard_map(
        body, mesh=mesh, in_specs=placed, out_specs=P("seq", "ch"), check_vma=False
    )
```

```python
import functools

import jax
import jax.numpy as jnp
import ml_dtypes
import numpy as np
from jax import lax
from jax.experimental import pallas as pl
from jax.experimental.pallas import tpu as pltpu
from jax.sharding import PartitionSpec as P

S = 32
Z = 8
C = 16
Q = 4
G = C // Q
T = 512
R = 64
K = 512
L = 128
KL = K // S
N = R * K
MESH = pl.DeviceIdType.MESH
VMEM = pltpu.VMEM
BF16, F32 = jnp.bfloat16, jnp.float32


def halves(table):
    table = np.asarray(table, np.float64)
    high = table.astype(ml_dtypes.bfloat16)
    low = (table - high.astype(np.float64)).astype(ml_dtypes.bfloat16)
    return high, low


@functools.lru_cache(None)
def tables():
    p, s = np.arange(R), np.arange(S)
    tau, kappa = np.arange(T), np.arange(K)
    cross = 2 * np.pi * np.outer(p, s) / R
    each = np.eye(Q)
    first = np.concatenate([np.cos(cross), -np.sin(cross)], 0)
    first = np.concatenate(halves(np.kron(each, first)), 1)
    turn = 2 * np.pi * np.outer(p, tau) / N
    inner = 2 * np.pi * (np.outer(kappa, tau) % K) / K
    inner = np.concatenate([np.cos(inner), np.sin(inner)], 1)
    inner_high, inner_low = halves(inner)
    last = np.concatenate([np.cos(cross).T, -np.sin(cross).T], 1) / N
    last_high, last_low = halves(np.kron(each, last))
    last = np.concatenate([last_high, last_low, last_high], 1)
    order = np.zeros((2 * R * G, 2 * R * G), ml_dtypes.bfloat16)
    for q in range(R):
        for g in range(G):
            for part in range(2):
                order[(q * G + g) * 2 + part, (g * 2 + part) * R + q] = 1
    return dict(
        order=order,
        first=first,
        turn=np.concatenate([np.cos(turn), np.sin(turn)], 0).astype(np.float32),
        inner=np.stack([inner_high, inner_low]),
        last=last,
    )


NAMES = ("order", "first", "turn", "inner", "last")


def dot(left, right, left_dim, right_dim):
    return lax.dot_general(
        left, right, (((left_dim,), (right_dim,)), ((), ())), preferred_element_type=F32
    )


def split(values):
    high = values.astype(BF16)
    return high, (values - high.astype(F32)).astype(BF16)


def lanes_at(start, size=L):
    return pl.ds(start if isinstance(start, int) else pl.multiple_of(start, L), size)


def chunk_lanes(g):
    return lanes_at(g * L)


def kernel(
    query_here, key_here, value_here, gain_here, spectra_here, weight_here, order_here, first_here,
    turn_here, inner_here, last_here, out, query, key, value, gain, spectra, order, first, turn,
    inner, last, gated_out, gated_in, filter_out, filter_in, conv_out, conv_in, share, weight, mixed,
    wide, rows, spectrum, product, back, turned, staging, loaded, sent_gated, sent_filter, sent_conv,
    sent_share, sent_weight, sent_ring, got_gated, got_filter, got_conv, got_share, got_weight,
    got_ring,
):
    me, level = lax.axis_index("seq"), lax.axis_index("ch")
    core, x, y = lax.rem(me, 2), lax.rem(me // 2, 4), me // 8
    sibling = me + 1 - 2 * core

    def peer(k):
        away_x = lax.rem(k, 4)
        away_y = lax.rem(k // 4 + away_x, 4)
        return (
            lax.rem(y + away_y, 4) * 8 + lax.rem(x + away_x, 4) * 2 + lax.rem(core + k // 16, 2)
        )

    def at_level(k):
        return lax.rem(level + k + Z, Z)

    def along_x(k):
        return y * 8 + lax.rem(x + k, 4) * 2 + core

    def along_y(k):
        return lax.rem(y + k, 4) * 8 + x * 2 + core

    barrier = pltpu.get_barrier_semaphore()

    @pl.loop(1, S)
    def _(k):
        pl.semaphore_signal(barrier, inc=1, device_id={"seq": peer(k)}, device_id_type=MESH)

    @pl.loop(1, Z)
    def _(k):
        pl.semaphore_signal(barrier, inc=1, device_id={"ch": at_level(k)}, device_id_type=MESH)

    share_here = weight_here.at[pl.ds(pl.multiple_of(me * C, C), C), :]
    loads = [
        pltpu.make_async_copy(source, target, loaded.at[i])
        for i, (source, target) in enumerate(
            (
                (key_here, key), (value_here, value), (spectra_here, spectra), (order_here, order),
                (share_here, share), (first_here, first), (turn_here, turn), (inner_here, inner),
                (last_here, last), (query_here, query), (gain_here, gain),
            )
        )
    ]
    for load in loads:
        load.start()

    def send(source, target, sent, got, **to):
        pltpu.make_async_remote_copy(
            src_ref=source, dst_ref=target, send_sem=sent, recv_sem=got, device_id=to,
            device_id_type=MESH,
        ).start()

    def send_all(source, target, sent, got):
        @pl.loop(1, S)
        def _(k):
            send(source.at[peer(k)], target.at[me], sent, got, seq=peer(k))

        target[me] = source[me]

    def wait(ref, sem):
        pltpu.make_async_copy(ref, ref, sem).wait()

    def arrive(target, sem):
        wait(target.at[pl.ds(0, S - 1)], sem)

    def share_lanes(k):
        return lanes_at(k * T, T)

    def spread_share():
        @pl.loop(1, Z)
        def _(k):
            to = at_level(k)
            send(
                share.at[:, share_lanes(to)], weight.at[level, me], sent_share, got_share, ch=to
            )

        weight[level, me] = share[:, share_lanes(level)]

    lower, upper = pl.ds(0, Z // 2), pl.ds(Z // 2, Z // 2)

    def weight_first():
        wait(weight.at[pl.ds(0, Z - 1), 0], got_share)

        @pl.loop(1, 4)
        def _(k):
            part = weight.at[lower, me]
            send(part, part, sent_weight.at[0], got_weight.at[0], seq=along_x(k))
            part = weight.at[upper, me]
            send(part, part, sent_weight.at[1], got_weight.at[1], seq=along_y(k))

    def weight_second():
        wait(weight.at[lower, pl.ds(0, 3)], got_weight.at[0])
        wait(weight.at[upper, pl.ds(0, 3)], got_weight.at[1])

        @pl.loop(1, 4)
        def _(k):
            @pl.loop(0, 4)
            def _(i):
                part = weight.at[lower, along_x(i)]
                send(part, part, sent_weight.at[2], got_weight.at[2], seq=along_y(k))
                part = weight.at[upper, along_y(i)]
                send(part, part, sent_weight.at[3], got_weight.at[3], seq=along_x(k))

    def weight_third():
        wait(weight.at[lower, pl.ds(0, 12)], got_weight.at[2])
        wait(weight.at[upper, pl.ds(0, 12)], got_weight.at[3])

        @pl.loop(0, S // 2)
        def _(i):
            part = weight.at[:, 2 * i + core]
            send(part, part, sent_weight.at[4], got_weight.at[4], seq=sibling)

    def weight_sent():
        wait(weight.at[pl.ds(0, Z - 1), 0], sent_share)
        wait(weight.at[lower, pl.ds(0, 3)], sent_weight.at[0])
        wait(weight.at[upper, pl.ds(0, 3)], sent_weight.at[1])
        wait(weight.at[lower, pl.ds(0, 12)], sent_weight.at[2])
        wait(weight.at[upper, pl.ds(0, 12)], sent_weight.at[3])
        wait(weight.at[:, pl.ds(0, S // 2)], sent_weight.at[4])

    def ring_part(way, hop, g, source):
        tokens = pl.ds(0, T)
        if hop == Z // 2:
            tokens = pl.ds(way * (T // 2), T // 2)
        lanes = lanes_at(source * T + g * L)
        return mixed.at[tokens, lanes]

    def ring_send(hop, g):
        for way, sign in enumerate((1, -1)):
            part = ring_part(way, hop, g, at_level(-sign * (hop - 1)))
            send(
                part, part, sent_ring.at[way, hop - 1, g], got_ring.at[way, hop - 1, g],
                ch=at_level(sign),
            )

    def ring_arrive(hop, g):
        for way, sign in enumerate((1, -1)):
            wait(ring_part(way, hop, g, at_level(-sign * hop)), got_ring.at[way, hop - 1, g])

    def forward(hop, g):
        ring_arrive(hop - 1, g)
        ring_send(hop, g)

    def prepare_gated(g):
        lanes = chunk_lanes(g)
        gated = (key[:, lanes].astype(F32) * value[:, lanes].astype(F32)).T
        for i in range(T // L):
            staging[pl.ds(i, L, stride=Q), :] = gated[:, i * L : (i + 1) * L]
        gated_out[g] = staging[...].astype(BF16).reshape(S, C, L)

    def prepare_filter():
        @pl.loop(0, KL)
        def _(k):
            block = spectra[pl.ds(pl.multiple_of(k * T, T), T), :]
            moved = dot(block, order[...], 0, 0)
            for g in range(G):
                wide[g, pl.ds(k, L, stride=KL), :] = moved[:, g * L : (g + 1) * L]

    def round_filter(g):
        filter_out[g] = wide[g].astype(BF16).reshape(S, Q, KL, L)

    def transform(g):
        staging[...] = gated_in[g].reshape(T, L).astype(F32)
        for c in range(Q):
            for i in range(T // L):
                part = staging[pl.ds(c * Q + i, S, stride=C), :].astype(BF16)
                for copy in range(2):
                    at = copy * L + c * S
                    turned[at : at + S, i * L : (i + 1) * L] = part
        back[:, :T] = dot(first[...], turned[: 2 * L, :], 1, 0)
        for c in range(Q):
            at = c * 2 * R
            real, imag = back[at : at + R, :T], back[at + R : at + 2 * R, :T]
            turned_real = (real * turn[:R] + imag * turn[R:]).astype(BF16)
            turned_imag = (imag * turn[:R] - real * turn[R:]).astype(BF16)
            rows[at : at + R, :T] = turned_real
            rows[at : at + R, T:] = turned_imag
            rows[at + R : at + 2 * R, :T] = turned_imag
            rows[at + R : at + 2 * R, T:] = -turned_real
        spectrum[g] = dot(inner[0], rows[...], 1, 1) + dot(inner[1], rows[...], 1, 1)

    def multiply(g):
        is_real = lax.broadcasted_iota(jnp.int32, (K, L), 1) < R
        for c in range(Q):
            lanes = slice(c * L, (c + 1) * L)
            response = filter_in[g, :, c].reshape(K, L).astype(F32)
            swapped = pltpu.roll(response, R, 1)
            value_c = spectrum[g, :, lanes]
            product[:, lanes] = (
                value_c * jnp.where(is_real, response, swapped)
                + pltpu.roll(value_c, R, 1) * jnp.where(is_real, -swapped, response)
            ).astype(BF16)

    def invert():
        back[...] = dot(product[...], inner[0], 0, 0) + dot(product[...], inner[1], 0, 0)

    def unturn():
        for c in range(Q):
            at = c * 2 * R
            real = back[at : at + R, :T] - back[at + R : at + 2 * R, T:]
            imag = back[at : at + R, T:] + back[at + R : at + 2 * R, :T]
            for at, part in (
                (at, real * turn[:R] - imag * turn[R:]),
                (at + R, real * turn[R:] + imag * turn[:R]),
            ):
                high, low = split(part)
                turned[at : at + R, :] = high
                turned[T + at : T + at + R, :] = high
                turned[2 * T + at : 2 * T + at + R, :] = low

    def finish(g):
        result = dot(last[...], turned[...], 1, 0)
        for c in range(Q):
            for i in range(T // L):
                staging[pl.ds(c * Q + i, S, stride=C), :] = result[
                    c * S : (c + 1) * S, i * L : (i + 1) * L
                ]
        conv_out[g] = staging[...].astype(BF16).reshape(S, C, L)

    def mix(g):
        staging[...] = conv_in[g].reshape(T, L).astype(F32)
        lanes = chunk_lanes(g)
        for i in range(T // L):
            tokens = slice(i * L, (i + 1) * L)
            convolved = staging[pl.ds(i, L, stride=Q), :].T
            gated = key[tokens, lanes].astype(F32) * value[tokens, lanes].astype(F32)
            mixed[tokens, lanes_at(level * T + g * L)] = (
                query[tokens, lanes].astype(F32) * (convolved + gain[:, lanes] * gated)
            ).astype(BF16)

    def project(source):
        return dot(mixed[:, share_lanes(source)], weight[source].reshape(T, T), 1, 0)

    def project_near():
        total = spectrum.at[0]
        total[...] = project(level)
        for k in (1, -1, 2, -2):
            total[...] += project(at_level(k))

    def project_far():
        total = spectrum[0] + project(at_level(3)) + project(at_level(-3))
        out[...] = (total + project(at_level(4))).astype(BF16)

    def send_gated(g):
        send_all(gated_out.at[g], gated_in.at[g], sent_gated.at[g], got_gated.at[g])

    def send_filter(g):
        send_all(filter_out.at[g], filter_in.at[g], sent_filter.at[g], got_filter.at[g])

    def convolve(g):
        arrive(filter_in.at[g], got_filter.at[g])
        multiply(g)
        invert()
        unturn()
        finish(g)
        send_all(conv_out.at[g], conv_in.at[g], sent_conv.at[g], got_conv.at[g])

    def combine(g):
        arrive(conv_in.at[g], got_conv.at[g])
        mix(g)
        ring_send(1, g)

    def begin(g):
        arrive(gated_in.at[g], got_gated.at[g])
        transform(g)

    def follow(g):
        send_gated(g)
        send_filter(g)

    for load in loads[:2]:
        load.wait()

    @pl.loop(0, G)
    def _(g):
        prepare_gated(g)

    for load in loads[2:4]:
        load.wait()
    prepare_filter()
    round_filter(0)
    pl.semaphore_wait(barrier, S + Z - 2)
    follow(0)
    round_filter(1)
    follow(1)
    for load in loads[4:]:
        load.wait()
    spread_share()
    round_filter(2)
    round_filter(3)

    begin(0)
    convolve(0)
    follow(2)
    begin(1)
    convolve(1)
    combine(0)
    follow(3)
    begin(2)
    convolve(2)
    forward(2, 0)
    combine(1)
    weight_first()
    begin(3)
    forward(3, 0)
    convolve(3)
    forward(2, 1)
    combine(2)
    forward(4, 0)
    weight_second()
    forward(3, 1)
    forward(2, 2)
    combine(3)
    forward(4, 1)
    forward(3, 2)
    forward(2, 3)
    forward(4, 2)
    forward(3, 3)
    weight_third()
    forward(4, 3)
    wait(weight.at[:, pl.ds(0, S // 2)], got_weight.at[4])
    project_near()
    for g in range(G):
        ring_arrive(Z // 2, g)
    project_far()
    weight_sent()
    for g in range(G):
        arrive(gated_out.at[g], sent_gated.at[g])
        arrive(filter_out.at[g], sent_filter.at[g])
        arrive(conv_out.at[g], sent_conv.at[g])
        for hop in range(1, Z // 2 + 1):
            for way in range(2):
                wait(ring_part(way, hop, g, 0), sent_ring.at[way, hop - 1, g])


def body(gate_query, gate_key, gate_value, skip_gain, filter_spectra, out_weight):
    tab = tables()
    spectra = filter_spectra.reshape(KL * R, 2, G, L).transpose(0, 2, 1, 3)
    dma = pltpu.SemaphoreType.DMA
    return pl.pallas_call(
        kernel,
        out_shape=jax.ShapeDtypeStruct((T, T), BF16),
        in_specs=[pl.BlockSpec(memory_space=pltpu.HBM)] * (6 + len(NAMES)),
        out_specs=pl.BlockSpec(memory_space=VMEM),
        scratch_shapes=[
            VMEM((T, T), BF16),
            VMEM((T, T), BF16),
            VMEM((T, T), BF16),
            VMEM((1, T), F32),
            VMEM((KL * R * G * 2, L), BF16),
            VMEM((2 * R * G, 2 * R * G), BF16),
            VMEM((T, 2 * L), BF16),
            VMEM((2 * R, T), F32),
            VMEM((2, K, 2 * T), BF16),
            VMEM((L, 3 * T), BF16),
            VMEM((G, S, C, L), BF16),
            VMEM((G, S, C, L), BF16),
            VMEM((G, S, Q, KL, L), BF16),
            VMEM((G, S, Q, KL, L), BF16),
            VMEM((G, S, C, L), BF16),
            VMEM((G, S, C, L), BF16),
            VMEM((C, Z * T), BF16),
            VMEM((Z, S, C, T), BF16),
            VMEM((T, Z * T), BF16),
            VMEM((G, L * KL, L), F32),
            VMEM((T, 2 * T), BF16),
            VMEM((G, K, T), F32),
            VMEM((K, T), BF16),
            VMEM((T, 2 * T), F32),
            VMEM((3 * T, T), BF16),
            VMEM((T, L), F32),
            dma((11,)),
            dma((G,)),
            dma((G,)),
            dma((G,)),
            dma(()),
            dma((5,)),
            dma((2, Z // 2, G)),
            dma((G,)),
            dma((G,)),
            dma((G,)),
            dma(()),
            dma((5,)),
            dma((2, Z // 2, G)),
        ],
        compiler_params=pltpu.CompilerParams(
            collective_id=0, has_side_effects=True, vmem_limit_bytes=58 << 20
        ),
        cost_estimate=pl.CostEstimate(flops=12 * 10**9, bytes_accessed=8 << 20, transcendentals=0),
    )(
        gate_query,
        gate_key,
        gate_value,
        skip_gain[None, :],
        spectra.reshape(KL * R * G * 2, L),
        out_weight,
        *(jnp.asarray(tab[name]) for name in NAMES),
    )


def solution(mesh):
    placed = (
        P("seq", "ch"),
        P("seq", "ch"),
        P("seq", "ch"),
        P("ch"),
        P("seq", None, "ch"),
        P("ch", None),
    )
    return jax.shard_map(
        body, mesh=mesh, in_specs=placed, out_specs=P("seq", "ch"), check_vma=False
    )
```

```python
import functools

import jax
import jax.numpy as jnp
import ml_dtypes
import numpy as np
from jax import lax
from jax.experimental import pallas as pl
from jax.experimental.pallas import tpu as pltpu
from jax.sharding import PartitionSpec as P

S = 32
Z = 8
C = 16
Q = 4
G = C // Q
T = 512
R = 64
K = 512
L = 128
KL = K // S
N = R * K
MESH = pl.DeviceIdType.MESH
VMEM = pltpu.VMEM
BF16, F32 = jnp.bfloat16, jnp.float32


def halves(table):
    table = np.asarray(table, np.float64)
    high = table.astype(ml_dtypes.bfloat16)
    low = (table - high.astype(np.float64)).astype(ml_dtypes.bfloat16)
    return high, low


@functools.lru_cache(None)
def tables():
    p, s = np.arange(R), np.arange(S)
    tau, kappa = np.arange(T), np.arange(K)
    cross = 2 * np.pi * np.outer(p, s) / R
    each = np.eye(Q)
    first = np.concatenate([np.cos(cross), -np.sin(cross)], 0)
    first = np.concatenate(halves(np.kron(each, first)), 1)
    turn = 2 * np.pi * np.outer(p, tau) / N
    inner = 2 * np.pi * (np.outer(kappa, tau) % K) / K
    inner = np.concatenate([np.cos(inner), np.sin(inner)], 1)
    inner_high, inner_low = halves(inner)
    last = np.concatenate([np.cos(cross).T, -np.sin(cross).T], 1) / N
    last_high, last_low = halves(np.kron(each, last))
    last = np.concatenate([last_high, last_low, last_high], 1)
    order = np.zeros((2 * R * G, 2 * R * G), ml_dtypes.bfloat16)
    for q in range(R):
        for g in range(G):
            for part in range(2):
                order[(q * G + g) * 2 + part, (g * 2 + part) * R + q] = 1
    return dict(
        order=order,
        first=first,
        turn=np.concatenate([np.cos(turn), np.sin(turn)], 0).astype(np.float32),
        inner=np.stack([inner_high, inner_low]),
        last=last,
    )


NAMES = ("order", "first", "turn", "inner", "last")


def dot(left, right, left_dim, right_dim):
    return lax.dot_general(
        left, right, (((left_dim,), (right_dim,)), ((), ())), preferred_element_type=F32
    )


def split(values):
    high = values.astype(BF16)
    return high, (values - high.astype(F32)).astype(BF16)


def lanes_at(start, size=L):
    return pl.ds(start if isinstance(start, int) else pl.multiple_of(start, L), size)


def chunk_lanes(g):
    return lanes_at(g * L)


def kernel(
    query_here, key_here, value_here, gain_here, spectra_here, weight_here, order_here, first_here,
    turn_here, inner_here, last_here, out, query, key, value, gain, spectra, order, first, turn,
    inner, last, gated_out, gated_in, filter_out, filter_in, conv_out, conv_in, share, weight, mixed,
    wide, rows, spectrum, product, back, turned, staging, loaded, sent_gated, sent_filter, sent_conv,
    sent_share, sent_weight, sent_ring, got_gated, got_filter, got_conv, got_share, got_weight,
    got_ring,
):
    me, level = lax.axis_index("seq"), lax.axis_index("ch")
    core, x, y = lax.rem(me, 2), lax.rem(me // 2, 4), me // 8
    sibling = me + 1 - 2 * core

    def peer(k):
        away_x = lax.rem(k, 4)
        away_y = lax.rem(k // 4 + away_x, 4)
        return (
            lax.rem(y + away_y, 4) * 8 + lax.rem(x + away_x, 4) * 2 + lax.rem(core + k // 16, 2)
        )

    def at_level(k):
        return lax.rem(level + k + Z, Z)

    def along_x(k):
        return y * 8 + lax.rem(x + k, 4) * 2 + core

    def along_y(k):
        return lax.rem(y + k, 4) * 8 + x * 2 + core

    barrier = pltpu.get_barrier_semaphore()

    @pl.loop(1, S)
    def _(k):
        pl.semaphore_signal(barrier, inc=1, device_id={"seq": peer(k)}, device_id_type=MESH)

    @pl.loop(1, Z)
    def _(k):
        pl.semaphore_signal(barrier, inc=1, device_id={"ch": at_level(k)}, device_id_type=MESH)

    share_here = weight_here.at[pl.ds(pl.multiple_of(me * C, C), C), :]
    loads = [
        pltpu.make_async_copy(source, target, loaded.at[i])
        for i, (source, target) in enumerate(
            (
                (key_here, key), (value_here, value), (spectra_here, spectra), (order_here, order),
                (share_here, share), (first_here, first), (turn_here, turn), (inner_here, inner),
                (last_here, last), (query_here, query), (gain_here, gain),
            )
        )
    ]
    for load in loads:
        load.start()

    def send(source, target, sent, got, **to):
        pltpu.make_async_remote_copy(
            src_ref=source, dst_ref=target, send_sem=sent, recv_sem=got, device_id=to,
            device_id_type=MESH,
        ).start()

    def send_all(source, target, sent, got):
        @pl.loop(1, S)
        def _(k):
            send(source.at[peer(k)], target.at[me], sent, got, seq=peer(k))

        target[me] = source[me]

    def wait(ref, sem):
        pltpu.make_async_copy(ref, ref, sem).wait()

    def arrive(target, sem):
        wait(target.at[pl.ds(0, S - 1)], sem)

    def share_lanes(k):
        return lanes_at(k * T, T)

    def spread_share():
        @pl.loop(1, Z)
        def _(k):
            to = at_level(k)
            send(
                share.at[:, share_lanes(to)], weight.at[level, me], sent_share, got_share, ch=to
            )

        weight[level, me] = share[:, share_lanes(level)]

    lower, upper = pl.ds(0, Z // 2), pl.ds(Z // 2, Z // 2)

    def weight_first():
        wait(weight.at[pl.ds(0, Z - 1), 0], got_share)

        @pl.loop(1, 4)
        def _(k):
            part = weight.at[lower, me]
            send(part, part, sent_weight.at[0], got_weight.at[0], seq=along_x(k))
            part = weight.at[upper, me]
            send(part, part, sent_weight.at[1], got_weight.at[1], seq=along_y(k))

    def weight_second():
        wait(weight.at[lower, pl.ds(0, 3)], got_weight.at[0])
        wait(weight.at[upper, pl.ds(0, 3)], got_weight.at[1])

        @pl.loop(1, 4)
        def _(k):
            @pl.loop(0, 4)
            def _(i):
                part = weight.at[lower, along_x(i)]
                send(part, part, sent_weight.at[2], got_weight.at[2], seq=along_y(k))
                part = weight.at[upper, along_y(i)]
                send(part, part, sent_weight.at[3], got_weight.at[3], seq=along_x(k))

    def weight_third():
        wait(weight.at[lower, pl.ds(0, 12)], got_weight.at[2])
        wait(weight.at[upper, pl.ds(0, 12)], got_weight.at[3])

        @pl.loop(0, S // 2)
        def _(i):
            part = weight.at[:, 2 * i + core]
            send(part, part, sent_weight.at[4], got_weight.at[4], seq=sibling)

    def weight_sent():
        wait(weight.at[pl.ds(0, Z - 1), 0], sent_share)
        wait(weight.at[lower, pl.ds(0, 3)], sent_weight.at[0])
        wait(weight.at[upper, pl.ds(0, 3)], sent_weight.at[1])
        wait(weight.at[lower, pl.ds(0, 12)], sent_weight.at[2])
        wait(weight.at[upper, pl.ds(0, 12)], sent_weight.at[3])
        wait(weight.at[:, pl.ds(0, S // 2)], sent_weight.at[4])

    def ring_part(way, hop, g, source):
        tokens = pl.ds(0, T)
        if hop == Z // 2:
            tokens = pl.ds(way * (T // 2), T // 2)
        lanes = lanes_at(source * T + g * L)
        return mixed.at[tokens, lanes]

    def ring_send(hop, g):
        for way, sign in enumerate((1, -1)):
            part = ring_part(way, hop, g, at_level(-sign * (hop - 1)))
            send(
                part, part, sent_ring.at[way, hop - 1, g], got_ring.at[way, hop - 1, g],
                ch=at_level(sign),
            )

    def ring_arrive(hop, g):
        for way, sign in enumerate((1, -1)):
            wait(ring_part(way, hop, g, at_level(-sign * hop)), got_ring.at[way, hop - 1, g])

    def forward(hop, g):
        ring_arrive(hop - 1, g)
        ring_send(hop, g)

    def prepare_gated(g):
        lanes = chunk_lanes(g)
        gated = (key[:, lanes].astype(F32) * value[:, lanes].astype(F32)).T
        for i in range(T // L):
            staging[pl.ds(i, L, stride=Q), :] = gated[:, i * L : (i + 1) * L]
        gated_out[g] = staging[...].astype(BF16).reshape(S, C, L)

    def prepare_filter():
        @pl.loop(0, KL)
        def _(k):
            block = spectra[pl.ds(pl.multiple_of(k * T, T), T), :]
            moved = dot(block, order[...], 0, 0)
            for g in range(G):
                wide[g, pl.ds(k, L, stride=KL), :] = moved[:, g * L : (g + 1) * L]

    def round_filter(g):
        filter_out[g] = wide[g].astype(BF16).reshape(S, Q, KL, L)

    def transform(g):
        staging[...] = gated_in[g].reshape(T, L).astype(F32)
        for c in range(Q):
            for i in range(T // L):
                part = staging[pl.ds(c * Q + i, S, stride=C), :].astype(BF16)
                for copy in range(2):
                    at = copy * L + c * S
                    turned[at : at + S, i * L : (i + 1) * L] = part
        back[:, :T] = dot(first[...], turned[: 2 * L, :], 1, 0)
        for c in range(Q):
            at = c * 2 * R
            real, imag = back[at : at + R, :T], back[at + R : at + 2 * R, :T]
            turned_real = (real * turn[:R] + imag * turn[R:]).astype(BF16)
            turned_imag = (imag * turn[:R] - real * turn[R:]).astype(BF16)
            rows[at : at + R, :T] = turned_real
            rows[at : at + R, T:] = turned_imag
            rows[at + R : at + 2 * R, :T] = turned_imag
            rows[at + R : at + 2 * R, T:] = -turned_real
        spectrum[g] = dot(inner[0], rows[...], 1, 1) + dot(inner[1], rows[...], 1, 1)

    def multiply(g):
        is_real = lax.broadcasted_iota(jnp.int32, (K, L), 1) < R
        for c in range(Q):
            lanes = slice(c * L, (c + 1) * L)
            response = filter_in[g, :, c].reshape(K, L).astype(F32)
            swapped = pltpu.roll(response, R, 1)
            value_c = spectrum[g, :, lanes]
            product[:, lanes] = (
                value_c * jnp.where(is_real, response, swapped)
                + pltpu.roll(value_c, R, 1) * jnp.where(is_real, -swapped, response)
            ).astype(BF16)

    def invert():
        back[...] = dot(product[...], inner[0], 0, 0) + dot(product[...], inner[1], 0, 0)

    def unturn():
        for c in range(Q):
            at = c * 2 * R
            real = back[at : at + R, :T] - back[at + R : at + 2 * R, T:]
            imag = back[at : at + R, T:] + back[at + R : at + 2 * R, :T]
            for at, part in (
                (at, real * turn[:R] - imag * turn[R:]),
                (at + R, real * turn[R:] + imag * turn[:R]),
            ):
                high, low = split(part)
                turned[at : at + R, :] = high
                turned[T + at : T + at + R, :] = high
                turned[2 * T + at : 2 * T + at + R, :] = low

    def finish(g):
        result = dot(last[...], turned[...], 1, 0)
        for c in range(Q):
            for i in range(T // L):
                staging[pl.ds(c * Q + i, S, stride=C), :] = result[
                    c * S : (c + 1) * S, i * L : (i + 1) * L
                ]
        conv_out[g] = staging[...].astype(BF16).reshape(S, C, L)

    def mix(g):
        staging[...] = conv_in[g].reshape(T, L).astype(F32)
        lanes = chunk_lanes(g)
        for i in range(T // L):
            tokens = slice(i * L, (i + 1) * L)
            convolved = staging[pl.ds(i, L, stride=Q), :].T
            gated = key[tokens, lanes].astype(F32) * value[tokens, lanes].astype(F32)
            mixed[tokens, lanes_at(level * T + g * L)] = (
                query[tokens, lanes].astype(F32) * (convolved + gain[:, lanes] * gated)
            ).astype(BF16)

    def project(source):
        return dot(mixed[:, share_lanes(source)], weight[source].reshape(T, T), 1, 0)

    def project_near():
        total = spectrum.at[0]
        total[...] = project(level)
        for k in (1, -1, 2, -2):
            total[...] += project(at_level(k))

    def project_next():
        total = spectrum.at[0]
        for k in (3, -3):
            total[...] += project(at_level(k))

    def project_last():
        out[...] = (spectrum[0] + project(at_level(4))).astype(BF16)

    def send_gated(g):
        send_all(gated_out.at[g], gated_in.at[g], sent_gated.at[g], got_gated.at[g])

    def send_filter(g):
        send_all(filter_out.at[g], filter_in.at[g], sent_filter.at[g], got_filter.at[g])

    def convolve(g):
        arrive(filter_in.at[g], got_filter.at[g])
        multiply(g)
        invert()
        unturn()
        finish(g)
        send_all(conv_out.at[g], conv_in.at[g], sent_conv.at[g], got_conv.at[g])

    def combine(g):
        arrive(conv_in.at[g], got_conv.at[g])
        mix(g)
        ring_send(1, g)

    def begin(g):
        arrive(gated_in.at[g], got_gated.at[g])
        transform(g)

    def follow(g):
        send_gated(g)
        send_filter(g)

    for load in loads[:2]:
        load.wait()

    @pl.loop(0, G)
    def _(g):
        prepare_gated(g)

    for load in loads[2:4]:
        load.wait()
    prepare_filter()
    round_filter(0)
    pl.semaphore_wait(barrier, S + Z - 2)
    follow(0)
    round_filter(1)
    follow(1)
    for load in loads[4:]:
        load.wait()
    spread_share()
    round_filter(2)
    round_filter(3)

    begin(0)
    convolve(0)
    follow(2)
    begin(1)
    convolve(1)
    combine(0)
    follow(3)
    begin(2)
    forward(2, 0)
    combine(1)
    convolve(2)
    weight_first()
    forward(3, 0)
    begin(3)
    forward(2, 1)
    convolve(3)
    combine(2)
    forward(3, 1)
    weight_second()
    forward(4, 0)
    combine(3)
    forward(4, 1)
    forward(2, 2)
    forward(2, 3)
    forward(3, 2)
    weight_third()
    forward(3, 3)
    forward(4, 2)
    wait(weight.at[:, pl.ds(0, S // 2)], got_weight.at[4])
    project_near()
    forward(4, 3)
    project_next()
    for g in range(G):
        ring_arrive(Z // 2, g)
    project_last()
    weight_sent()
    for g in range(G):
        arrive(gated_out.at[g], sent_gated.at[g])
        arrive(filter_out.at[g], sent_filter.at[g])
        arrive(conv_out.at[g], sent_conv.at[g])
        for hop in range(1, Z // 2 + 1):
            for way in range(2):
                wait(ring_part(way, hop, g, 0), sent_ring.at[way, hop - 1, g])


def body(gate_query, gate_key, gate_value, skip_gain, filter_spectra, out_weight):
    tab = tables()
    spectra = filter_spectra.reshape(KL * R, 2, G, L).transpose(0, 2, 1, 3)
    dma = pltpu.SemaphoreType.DMA
    return pl.pallas_call(
        kernel,
        out_shape=jax.ShapeDtypeStruct((T, T), BF16),
        in_specs=[pl.BlockSpec(memory_space=pltpu.HBM)] * (6 + len(NAMES)),
        out_specs=pl.BlockSpec(memory_space=VMEM),
        scratch_shapes=[
            VMEM((T, T), BF16),
            VMEM((T, T), BF16),
            VMEM((T, T), BF16),
            VMEM((1, T), F32),
            VMEM((KL * R * G * 2, L), BF16),
            VMEM((2 * R * G, 2 * R * G), BF16),
            VMEM((T, 2 * L), BF16),
            VMEM((2 * R, T), F32),
            VMEM((2, K, 2 * T), BF16),
            VMEM((L, 3 * T), BF16),
            VMEM((G, S, C, L), BF16),
            VMEM((G, S, C, L), BF16),
            VMEM((G, S, Q, KL, L), BF16),
            VMEM((G, S, Q, KL, L), BF16),
            VMEM((G, S, C, L), BF16),
            VMEM((G, S, C, L), BF16),
            VMEM((C, Z * T), BF16),
            VMEM((Z, S, C, T), BF16),
            VMEM((T, Z * T), BF16),
            VMEM((G, L * KL, L), F32),
            VMEM((T, 2 * T), BF16),
            VMEM((G, K, T), F32),
            VMEM((K, T), BF16),
            VMEM((T, 2 * T), F32),
            VMEM((3 * T, T), BF16),
            VMEM((T, L), F32),
            dma((11,)),
            dma((G,)),
            dma((G,)),
            dma((G,)),
            dma(()),
            dma((5,)),
            dma((2, Z // 2, G)),
            dma((G,)),
            dma((G,)),
            dma((G,)),
            dma(()),
            dma((5,)),
            dma((2, Z // 2, G)),
        ],
        compiler_params=pltpu.CompilerParams(
            collective_id=0, has_side_effects=True, vmem_limit_bytes=48 << 20
        ),
        cost_estimate=pl.CostEstimate(flops=12 * 10**9, bytes_accessed=8 << 20, transcendentals=0),
    )(
        gate_query,
        gate_key,
        gate_value,
        skip_gain[None, :],
        spectra.reshape(KL * R * G * 2, L),
        out_weight,
        *(jnp.asarray(tab[name]) for name in NAMES),
    )


def solution(mesh):
    placed = (
        P("seq", "ch"),
        P("seq", "ch"),
        P("seq", "ch"),
        P("ch"),
        P("seq", None, "ch"),
        P("ch", None),
    )
    return jax.shard_map(
        body, mesh=mesh, in_specs=placed, out_specs=P("seq", "ch"), check_vma=False
    )
```

```python
import functools

import jax
import jax.numpy as jnp
import ml_dtypes
import numpy as np
from jax import lax
from jax.experimental import pallas as pl
from jax.experimental.pallas import tpu as pltpu
from jax.sharding import PartitionSpec as P

S = 32
Z = 8
C = 16
Q = 4
G = C // Q
T = 512
R = 64
K = 512
L = 128
KL = K // S
N = R * K
MESH = pl.DeviceIdType.MESH
VMEM = pltpu.VMEM
BF16, F32 = jnp.bfloat16, jnp.float32


def halves(table):
    table = np.asarray(table, np.float64)
    high = table.astype(ml_dtypes.bfloat16)
    low = (table - high.astype(np.float64)).astype(ml_dtypes.bfloat16)
    return high, low


@functools.lru_cache(None)
def tables():
    p, s = np.arange(R), np.arange(S)
    tau, kappa = np.arange(T), np.arange(K)
    cross = 2 * np.pi * np.outer(p, s) / R
    each = np.eye(Q)
    first = np.concatenate([np.cos(cross), -np.sin(cross)], 0)
    first = np.concatenate(halves(np.kron(each, first)), 1)
    turn = 2 * np.pi * np.outer(p, tau) / N
    inner = 2 * np.pi * (np.outer(kappa, tau) % K) / K
    inner = np.concatenate([np.cos(inner), np.sin(inner)], 1)
    inner_high, inner_low = halves(inner)
    last = np.concatenate([np.cos(cross).T, -np.sin(cross).T], 1) / N
    last_high, last_low = halves(np.kron(each, last))
    last = np.concatenate([last_high, last_low, last_high], 1)
    order = np.zeros((2 * R * G, 2 * R * G), ml_dtypes.bfloat16)
    for q in range(R):
        for g in range(G):
            for part in range(2):
                order[(q * G + g) * 2 + part, (g * 2 + part) * R + q] = 1
    return dict(
        order=order,
        first=first,
        turn=np.concatenate([np.cos(turn), np.sin(turn)], 0).astype(np.float32),
        inner=np.stack([inner_high, inner_low]),
        last=last,
    )


NAMES = ("order", "first", "turn", "inner", "last")


def dot(left, right, left_dim, right_dim):
    return lax.dot_general(
        left, right, (((left_dim,), (right_dim,)), ((), ())), preferred_element_type=F32
    )


def split(values):
    high = values.astype(BF16)
    return high, (values - high.astype(F32)).astype(BF16)


def lanes_at(start, size=L):
    return pl.ds(start if isinstance(start, int) else pl.multiple_of(start, L), size)


def chunk_lanes(g):
    return lanes_at(g * L)


def kernel(
    query_here, key_here, value_here, gain_here, spectra_here, weight_here, order_here, first_here,
    turn_here, inner_here, last_here, out, query, key, value, gain, spectra, order, first, turn,
    inner, last, gated_out, gated_in, filter_out, filter_in, conv_out, conv_in, share, weight, mixed,
    wide, rows, spectrum, product, back, turned, staging, loaded, sent_gated, sent_filter, sent_conv,
    sent_share, sent_weight, sent_ring, got_gated, got_filter, got_conv, got_share, got_weight,
    got_ring,
):
    me, level = lax.axis_index("seq"), lax.axis_index("ch")
    core, x, y = lax.rem(me, 2), lax.rem(me // 2, 4), me // 8
    sibling = me + 1 - 2 * core

    def peer(k):
        away_x = lax.rem(k, 4)
        away_y = lax.rem(k // 4 + away_x, 4)
        return (
            lax.rem(y + away_y, 4) * 8 + lax.rem(x + away_x, 4) * 2 + lax.rem(core + k // 16, 2)
        )

    def at_level(k):
        return lax.rem(level + k + Z, Z)

    def along_x(k):
        return y * 8 + lax.rem(x + k, 4) * 2 + core

    def along_y(k):
        return lax.rem(y + k, 4) * 8 + x * 2 + core

    barrier = pltpu.get_barrier_semaphore()

    @pl.loop(1, S)
    def _(k):
        pl.semaphore_signal(barrier, inc=1, device_id={"seq": peer(k)}, device_id_type=MESH)

    @pl.loop(1, Z)
    def _(k):
        pl.semaphore_signal(barrier, inc=1, device_id={"ch": at_level(k)}, device_id_type=MESH)

    share_here = weight_here.at[pl.ds(pl.multiple_of(me * C, C), C), :]
    loads = [
        pltpu.make_async_copy(source, target, loaded.at[i])
        for i, (source, target) in enumerate(
            (
                (key_here, key), (value_here, value), (spectra_here, spectra), (order_here, order),
                (share_here, share), (first_here, first), (turn_here, turn), (inner_here, inner),
                (last_here, last), (query_here, query), (gain_here, gain),
            )
        )
    ]
    for load in loads:
        load.start()

    def send(source, target, sent, got, **to):
        pltpu.make_async_remote_copy(
            src_ref=source, dst_ref=target, send_sem=sent, recv_sem=got, device_id=to,
            device_id_type=MESH,
        ).start()

    def send_all(source, target, sent, got):
        @pl.loop(1, S)
        def _(k):
            send(source.at[peer(k)], target.at[me], sent, got, seq=peer(k))

        target[me] = source[me]

    def wait(ref, sem):
        pltpu.make_async_copy(ref, ref, sem).wait()

    def arrive(target, sem):
        wait(target.at[pl.ds(0, S - 1)], sem)

    def share_lanes(k):
        return lanes_at(k * T, T)

    def spread_share():
        @pl.loop(1, Z)
        def _(k):
            to = at_level(k)
            send(
                share.at[:, share_lanes(to)], weight.at[level, me], sent_share, got_share, ch=to
            )

        weight[level, me] = share[:, share_lanes(level)]

    lower, upper = pl.ds(0, Z // 2), pl.ds(Z // 2, Z // 2)

    def weight_first():
        wait(weight.at[pl.ds(0, Z - 1), 0], got_share)

        @pl.loop(1, 4)
        def _(k):
            part = weight.at[lower, me]
            send(part, part, sent_weight.at[0], got_weight.at[0], seq=along_x(k))
            part = weight.at[upper, me]
            send(part, part, sent_weight.at[1], got_weight.at[1], seq=along_y(k))

    def weight_second():
        wait(weight.at[lower, pl.ds(0, 3)], got_weight.at[0])
        wait(weight.at[upper, pl.ds(0, 3)], got_weight.at[1])

        @pl.loop(1, 4)
        def _(k):
            @pl.loop(0, 4)
            def _(i):
                part = weight.at[lower, along_x(i)]
                send(part, part, sent_weight.at[2], got_weight.at[2], seq=along_y(k))
                part = weight.at[upper, along_y(i)]
                send(part, part, sent_weight.at[3], got_weight.at[3], seq=along_x(k))

    def weight_third():
        wait(weight.at[lower, pl.ds(0, 12)], got_weight.at[2])
        wait(weight.at[upper, pl.ds(0, 12)], got_weight.at[3])

        @pl.loop(0, S // 2)
        def _(i):
            part = weight.at[:, 2 * i + core]
            send(part, part, sent_weight.at[4], got_weight.at[4], seq=sibling)

    def weight_sent():
        wait(weight.at[pl.ds(0, Z - 1), 0], sent_share)
        wait(weight.at[lower, pl.ds(0, 3)], sent_weight.at[0])
        wait(weight.at[upper, pl.ds(0, 3)], sent_weight.at[1])
        wait(weight.at[lower, pl.ds(0, 12)], sent_weight.at[2])
        wait(weight.at[upper, pl.ds(0, 12)], sent_weight.at[3])
        wait(weight.at[:, pl.ds(0, S // 2)], sent_weight.at[4])

    def ring_part(way, hop, g, source):
        tokens = pl.ds(0, T)
        if hop == Z // 2:
            tokens = pl.ds(way * (T // 2), T // 2)
        lanes = lanes_at(source * T + g * L)
        return mixed.at[tokens, lanes]

    def ring_send(hop, g):
        for way, sign in enumerate((1, -1)):
            part = ring_part(way, hop, g, at_level(-sign * (hop - 1)))
            send(
                part, part, sent_ring.at[way, hop - 1, g], got_ring.at[way, hop - 1, g],
                ch=at_level(sign),
            )

    def ring_arrive(hop, g):
        for way, sign in enumerate((1, -1)):
            wait(ring_part(way, hop, g, at_level(-sign * hop)), got_ring.at[way, hop - 1, g])

    def forward(hop, g):
        ring_arrive(hop - 1, g)
        ring_send(hop, g)

    def prepare_gated(g):
        lanes = chunk_lanes(g)
        gated = (key[:, lanes].astype(F32) * value[:, lanes].astype(F32)).T
        for i in range(T // L):
            staging[pl.ds(i, L, stride=Q), :] = gated[:, i * L : (i + 1) * L]
        gated_out[g] = staging[...].astype(BF16).reshape(S, C, L)

    def prepare_filter():
        @pl.loop(0, KL)
        def _(k):
            block = spectra[pl.ds(pl.multiple_of(k * T, T), T), :]
            moved = dot(block, order[...], 0, 0)
            for g in range(G):
                wide[g, pl.ds(k, L, stride=KL), :] = moved[:, g * L : (g + 1) * L]

    def round_filter(g):
        filter_out[g] = wide[g].astype(BF16).reshape(S, Q, KL, L)

    def transform(g):
        staging[...] = gated_in[g].reshape(T, L).astype(F32)
        for c in range(Q):
            for i in range(T // L):
                part = staging[pl.ds(c * Q + i, S, stride=C), :].astype(BF16)
                for copy in range(2):
                    at = copy * L + c * S
                    turned[at : at + S, i * L : (i + 1) * L] = part
        back[:, :T] = dot(first[...], turned[: 2 * L, :], 1, 0)
        for c in range(Q):
            at = c * 2 * R
            real, imag = back[at : at + R, :T], back[at + R : at + 2 * R, :T]
            turned_real = (real * turn[:R] + imag * turn[R:]).astype(BF16)
            turned_imag = (imag * turn[:R] - real * turn[R:]).astype(BF16)
            rows[at : at + R, :T] = turned_real
            rows[at : at + R, T:] = turned_imag
            rows[at + R : at + 2 * R, :T] = turned_imag
            rows[at + R : at + 2 * R, T:] = -turned_real
        spectrum[g] = dot(inner[0], rows[...], 1, 1) + dot(inner[1], rows[...], 1, 1)

    def multiply(g):
        is_real = lax.broadcasted_iota(jnp.int32, (K, L), 1) < R
        for c in range(Q):
            lanes = slice(c * L, (c + 1) * L)
            response = filter_in[g, :, c].reshape(K, L).astype(F32)
            swapped = pltpu.roll(response, R, 1)
            value_c = spectrum[g, :, lanes]
            product[:, lanes] = (
                value_c * jnp.where(is_real, response, swapped)
                + pltpu.roll(value_c, R, 1) * jnp.where(is_real, -swapped, response)
            ).astype(BF16)

    def invert():
        back[...] = dot(product[...], inner[0], 0, 0) + dot(product[...], inner[1], 0, 0)

    def unturn():
        for c in range(Q):
            at = c * 2 * R
            real = back[at : at + R, :T] - back[at + R : at + 2 * R, T:]
            imag = back[at : at + R, T:] + back[at + R : at + 2 * R, :T]
            for at, part in (
                (at, real * turn[:R] - imag * turn[R:]),
                (at + R, real * turn[R:] + imag * turn[:R]),
            ):
                high, low = split(part)
                turned[at : at + R, :] = high
                turned[T + at : T + at + R, :] = high
                turned[2 * T + at : 2 * T + at + R, :] = low

    def finish(g):
        result = dot(last[...], turned[...], 1, 0)
        for c in range(Q):
            for i in range(T // L):
                staging[pl.ds(c * Q + i, S, stride=C), :] = result[
                    c * S : (c + 1) * S, i * L : (i + 1) * L
                ]
        conv_out[g] = staging[...].astype(BF16).reshape(S, C, L)

    def mix(g):
        staging[...] = conv_in[g].reshape(T, L).astype(F32)
        lanes = chunk_lanes(g)
        for i in range(T // L):
            tokens = slice(i * L, (i + 1) * L)
            convolved = staging[pl.ds(i, L, stride=Q), :].T
            gated = key[tokens, lanes].astype(F32) * value[tokens, lanes].astype(F32)
            mixed[tokens, lanes_at(level * T + g * L)] = (
                query[tokens, lanes].astype(F32) * (convolved + gain[:, lanes] * gated)
            ).astype(BF16)

    def project(source):
        return dot(mixed[:, share_lanes(source)], weight[source].reshape(T, T), 1, 0)

    def project_near():
        total = spectrum.at[0]
        total[...] = project(level)
        for k in (1, -1, 2, -2):
            total[...] += project(at_level(k))

    def project_next():
        total = spectrum.at[0]
        for k in (3, -3):
            total[...] += project(at_level(k))

    def project_last():
        out[...] = (spectrum[0] + project(at_level(4))).astype(BF16)

    def send_gated(g):
        send_all(gated_out.at[g], gated_in.at[g], sent_gated.at[g], got_gated.at[g])

    def send_filter(g):
        send_all(filter_out.at[g], filter_in.at[g], sent_filter.at[g], got_filter.at[g])

    def convolve(g):
        arrive(filter_in.at[g], got_filter.at[g])
        multiply(g)
        invert()
        unturn()
        finish(g)
        send_all(conv_out.at[g], conv_in.at[g], sent_conv.at[g], got_conv.at[g])

    def combine(g):
        arrive(conv_in.at[g], got_conv.at[g])
        mix(g)
        ring_send(1, g)

    def begin(g):
        arrive(gated_in.at[g], got_gated.at[g])
        transform(g)

    def follow(g):
        send_gated(g)
        send_filter(g)

    for load in loads[:2]:
        load.wait()

    @pl.loop(0, G)
    def _(g):
        prepare_gated(g)

    for load in loads[2:4]:
        load.wait()
    prepare_filter()
    round_filter(0)
    pl.semaphore_wait(barrier, S + Z - 2)
    follow(0)
    round_filter(1)
    follow(1)
    for load in loads[4:]:
        load.wait()
    spread_share()
    round_filter(2)
    round_filter(3)

    begin(0)
    convolve(0)
    follow(2)
    begin(1)
    convolve(1)
    combine(0)
    follow(3)
    begin(2)
    forward(2, 0)
    combine(1)
    convolve(2)
    weight_first()
    forward(3, 0)
    begin(3)
    forward(2, 1)
    convolve(3)
    combine(2)
    forward(3, 1)
    weight_second()
    forward(4, 0)
    combine(3)
    forward(4, 1)
    forward(2, 2)
    forward(2, 3)
    forward(3, 2)
    weight_third()
    forward(3, 3)
    forward(4, 2)
    wait(weight.at[:, pl.ds(0, S // 2)], got_weight.at[4])
    project_near()
    forward(4, 3)
    project_next()
    for g in range(G):
        ring_arrive(Z // 2, g)
    project_last()
    weight_sent()
    for g in range(G):
        arrive(gated_out.at[g], sent_gated.at[g])
        arrive(filter_out.at[g], sent_filter.at[g])
        arrive(conv_out.at[g], sent_conv.at[g])
        for hop in range(1, Z // 2 + 1):
            for way in range(2):
                wait(ring_part(way, hop, g, 0), sent_ring.at[way, hop - 1, g])


def body(gate_query, gate_key, gate_value, skip_gain, filter_spectra, out_weight):
    tab = tables()
    spectra = filter_spectra.reshape(KL * R, 2, G, L).transpose(0, 2, 1, 3)
    dma = pltpu.SemaphoreType.DMA
    return pl.pallas_call(
        kernel,
        out_shape=jax.ShapeDtypeStruct((T, T), BF16),
        in_specs=[pl.BlockSpec(memory_space=pltpu.HBM)] * (6 + len(NAMES)),
        out_specs=pl.BlockSpec(memory_space=VMEM),
        scratch_shapes=[
            VMEM((T, T), BF16),
            VMEM((T, T), BF16),
            VMEM((T, T), BF16),
            VMEM((1, T), F32),
            VMEM((KL * R * G * 2, L), BF16),
            VMEM((2 * R * G, 2 * R * G), BF16),
            VMEM((T, 2 * L), BF16),
            VMEM((2 * R, T), F32),
            VMEM((2, K, 2 * T), BF16),
            VMEM((L, 3 * T), BF16),
            VMEM((G, S, C, L), BF16),
            VMEM((G, S, C, L), BF16),
            VMEM((G, S, Q, KL, L), BF16),
            VMEM((G, S, Q, KL, L), BF16),
            VMEM((G, S, C, L), BF16),
            VMEM((G, S, C, L), BF16),
            VMEM((C, Z * T), BF16),
            VMEM((Z, S, C, T), BF16),
            VMEM((T, Z * T), BF16),
            VMEM((G, L * KL, L), F32),
            VMEM((T, 2 * T), BF16),
            VMEM((G, K, T), F32),
            VMEM((K, T), BF16),
            VMEM((T, 2 * T), F32),
            VMEM((3 * T, T), BF16),
            VMEM((T, L), F32),
            dma((11,)),
            dma((G,)),
            dma((G,)),
            dma((G,)),
            dma(()),
            dma((5,)),
            dma((2, Z // 2, G)),
            dma((G,)),
            dma((G,)),
            dma((G,)),
            dma(()),
            dma((5,)),
            dma((2, Z // 2, G)),
        ],
        compiler_params=pltpu.CompilerParams(
            collective_id=0, has_side_effects=True, vmem_limit_bytes=58 << 20
        ),
        cost_estimate=pl.CostEstimate(flops=12 * 10**9, bytes_accessed=8 << 20, transcendentals=0),
    )(
        gate_query,
        gate_key,
        gate_value,
        skip_gain[None, :],
        spectra.reshape(KL * R * G * 2, L),
        out_weight,
        *(jnp.asarray(tab[name]) for name in NAMES),
    )


def solution(mesh):
    placed = (
        P("seq", "ch"),
        P("seq", "ch"),
        P("seq", "ch"),
        P("ch"),
        P("seq", None, "ch"),
        P("ch", None),
    )
    return jax.shard_map(
        body, mesh=mesh, in_specs=placed, out_specs=P("seq", "ch"), check_vma=False
    )
```

```python
import functools

import jax
import jax.numpy as jnp
import ml_dtypes
import numpy as np
from jax import lax
from jax.experimental import pallas as pl
from jax.experimental.pallas import tpu as pltpu
from jax.sharding import PartitionSpec as P

S = 32
Z = 8
C = 16
Q = 4
G = C // Q
T = 512
R = 64
K = 512
L = 128
KL = K // S
N = R * K
MESH = pl.DeviceIdType.MESH
VMEM = pltpu.VMEM
BF16, F32 = jnp.bfloat16, jnp.float32


def halves(table):
    table = np.asarray(table, np.float64)
    high = table.astype(ml_dtypes.bfloat16)
    low = (table - high.astype(np.float64)).astype(ml_dtypes.bfloat16)
    return high, low


@functools.lru_cache(None)
def tables():
    p, s = np.arange(R), np.arange(S)
    tau, kappa = np.arange(T), np.arange(K)
    cross = 2 * np.pi * np.outer(p, s) / R
    each = np.eye(Q)
    first = np.concatenate([np.cos(cross), -np.sin(cross)], 0)
    first = np.concatenate(halves(np.kron(each, first)), 1)
    turn = 2 * np.pi * np.outer(p, tau) / N
    inner = 2 * np.pi * (np.outer(kappa, tau) % K) / K
    inner = np.concatenate([np.cos(inner), np.sin(inner)], 1)
    inner_high, inner_low = halves(inner)
    last = np.concatenate([np.cos(cross).T, -np.sin(cross).T], 1) / N
    last_high, last_low = halves(np.kron(each, last))
    last = np.concatenate([last_high, last_low, last_high], 1)
    order = np.zeros((2 * R * G, 2 * R * G), ml_dtypes.bfloat16)
    for q in range(R):
        for g in range(G):
            for part in range(2):
                order[(q * G + g) * 2 + part, (g * 2 + part) * R + q] = 1
    return dict(
        order=order,
        first=first,
        turn=np.concatenate([np.cos(turn), np.sin(turn)], 0).astype(np.float32),
        inner=np.stack([inner_high, inner_low]),
        last=last,
    )


NAMES = ("order", "first", "turn", "inner", "last")


def dot(left, right, left_dim, right_dim):
    return lax.dot_general(
        left, right, (((left_dim,), (right_dim,)), ((), ())), preferred_element_type=F32
    )


def split(values):
    high = values.astype(BF16)
    return high, (values - high.astype(F32)).astype(BF16)


def lanes_at(start, size=L):
    return pl.ds(start if isinstance(start, int) else pl.multiple_of(start, L), size)


def chunk_lanes(g):
    return lanes_at(g * L)


def kernel(
    query_here, key_here, value_here, gain_here, spectra_here, weight_here, order_here, first_here,
    turn_here, inner_here, last_here, out, query, key, value, gain, spectra, order, first, turn,
    inner, last, gated_out, gated_in, filter_out, filter_in, conv_out, conv_in, share, weight, mixed,
    wide, rows, spectrum, product, back, turned, staging, loaded, sent_gated, sent_filter, sent_conv,
    sent_share, sent_weight, sent_ring, got_gated, got_filter, got_conv, got_share, got_weight,
    got_ring,
):
    me, level = lax.axis_index("seq"), lax.axis_index("ch")
    core, x, y = lax.rem(me, 2), lax.rem(me // 2, 4), me // 8
    sibling = me + 1 - 2 * core

    def peer(k):
        away_x = lax.rem(k, 4)
        away_y = lax.rem(k // 4 + away_x, 4)
        return (
            lax.rem(y + away_y, 4) * 8 + lax.rem(x + away_x, 4) * 2 + lax.rem(core + k // 16, 2)
        )

    def at_level(k):
        return lax.rem(level + k + Z, Z)

    def along_x(k):
        return y * 8 + lax.rem(x + k, 4) * 2 + core

    def along_y(k):
        return lax.rem(y + k, 4) * 8 + x * 2 + core

    barrier = pltpu.get_barrier_semaphore()

    @pl.loop(1, S)
    def _(k):
        pl.semaphore_signal(barrier, inc=1, device_id={"seq": peer(k)}, device_id_type=MESH)

    @pl.loop(1, Z)
    def _(k):
        pl.semaphore_signal(barrier, inc=1, device_id={"ch": at_level(k)}, device_id_type=MESH)

    share_here = weight_here.at[pl.ds(pl.multiple_of(me * C, C), C), :]
    loads = [
        pltpu.make_async_copy(source, target, loaded.at[i])
        for i, (source, target) in enumerate(
            (
                (key_here, key), (value_here, value), (spectra_here, spectra), (order_here, order),
                (share_here, share), (first_here, first), (turn_here, turn), (inner_here, inner),
                (last_here, last), (query_here, query), (gain_here, gain),
            )
        )
    ]
    for load in loads:
        load.start()

    def send(source, target, sent, got, **to):
        pltpu.make_async_remote_copy(
            src_ref=source, dst_ref=target, send_sem=sent, recv_sem=got, device_id=to,
            device_id_type=MESH,
        ).start()

    def send_all(source, target, sent, got):
        @pl.loop(1, S)
        def _(k):
            send(source.at[peer(k)], target.at[me], sent, got, seq=peer(k))

        target[me] = source[me]

    def wait(ref, sem):
        pltpu.make_async_copy(ref, ref, sem).wait()

    def arrive(target, sem):
        wait(target.at[pl.ds(0, S - 1)], sem)

    def share_lanes(k):
        return lanes_at(k * T, T)

    def spread_share():
        @pl.loop(1, Z)
        def _(k):
            to = at_level(k)
            send(
                share.at[:, share_lanes(to)], weight.at[level, me], sent_share, got_share, ch=to
            )

        weight[level, me] = share[:, share_lanes(level)]

    lower, upper = pl.ds(0, Z // 2), pl.ds(Z // 2, Z // 2)

    def weight_first():
        wait(weight.at[pl.ds(0, Z - 1), 0], got_share)

        @pl.loop(1, 4)
        def _(k):
            part = weight.at[lower, me]
            send(part, part, sent_weight.at[0], got_weight.at[0], seq=along_x(k))
            part = weight.at[upper, me]
            send(part, part, sent_weight.at[1], got_weight.at[1], seq=along_y(k))

    def weight_second():
        wait(weight.at[lower, pl.ds(0, 3)], got_weight.at[0])
        wait(weight.at[upper, pl.ds(0, 3)], got_weight.at[1])

        @pl.loop(1, 4)
        def _(k):
            @pl.loop(0, 4)
            def _(i):
                part = weight.at[lower, along_x(i)]
                send(part, part, sent_weight.at[2], got_weight.at[2], seq=along_y(k))
                part = weight.at[upper, along_y(i)]
                send(part, part, sent_weight.at[3], got_weight.at[3], seq=along_x(k))

    def weight_third():
        wait(weight.at[lower, pl.ds(0, 12)], got_weight.at[2])
        wait(weight.at[upper, pl.ds(0, 12)], got_weight.at[3])

        @pl.loop(0, S // 2)
        def _(i):
            part = weight.at[:, 2 * i + core]
            send(part, part, sent_weight.at[4], got_weight.at[4], seq=sibling)

    def weight_sent():
        wait(weight.at[pl.ds(0, Z - 1), 0], sent_share)
        wait(weight.at[lower, pl.ds(0, 3)], sent_weight.at[0])
        wait(weight.at[upper, pl.ds(0, 3)], sent_weight.at[1])
        wait(weight.at[lower, pl.ds(0, 12)], sent_weight.at[2])
        wait(weight.at[upper, pl.ds(0, 12)], sent_weight.at[3])
        wait(weight.at[:, pl.ds(0, S // 2)], sent_weight.at[4])

    def ring_parts(way, hop):
        return (way,) if hop == Z // 2 else (0, 1)

    def ring_part(part, g, source):
        return mixed.at[pl.ds(part * (T // 2), T // 2), lanes_at(source * T + g * L)]

    def ring_send(way, hop, g, part):
        sign = 1 - 2 * way
        piece = ring_part(part, g, at_level(-sign * (hop - 1)))
        send(
            piece, piece, sent_ring.at[way, hop - 1, g, part], got_ring.at[way, hop - 1, g, part],
            ch=at_level(sign),
        )

    def ring_arrive(way, hop, g, part):
        sign = 1 - 2 * way
        wait(ring_part(part, g, at_level(-sign * hop)), got_ring.at[way, hop - 1, g, part])

    def forward(hop, g):
        for part in range(2):
            for way in range(2):
                if part in ring_parts(way, hop - 1):
                    ring_arrive(way, hop - 1, g, part)
                if part in ring_parts(way, hop):
                    ring_send(way, hop, g, part)

    def prepare_gated(g):
        lanes = chunk_lanes(g)
        gated = (key[:, lanes].astype(F32) * value[:, lanes].astype(F32)).T
        for i in range(T // L):
            staging[pl.ds(i, L, stride=Q), :] = gated[:, i * L : (i + 1) * L]
        gated_out[g] = staging[...].astype(BF16).reshape(S, C, L)

    def prepare_filter():
        @pl.loop(0, KL)
        def _(k):
            block = spectra[pl.ds(pl.multiple_of(k * T, T), T), :]
            moved = dot(block, order[...], 0, 0)
            for g in range(G):
                wide[g, pl.ds(k, L, stride=KL), :] = moved[:, g * L : (g + 1) * L]

    def round_filter(g):
        filter_out[g] = wide[g].astype(BF16).reshape(S, Q, KL, L)

    def transform(g):
        staging[...] = gated_in[g].reshape(T, L).astype(F32)
        for c in range(Q):
            for i in range(T // L):
                part = staging[pl.ds(c * Q + i, S, stride=C), :].astype(BF16)
                for copy in range(2):
                    at = copy * L + c * S
                    turned[at : at + S, i * L : (i + 1) * L] = part
        back[:, :T] = dot(first[...], turned[: 2 * L, :], 1, 0)
        for c in range(Q):
            at = c * 2 * R
            real, imag = back[at : at + R, :T], back[at + R : at + 2 * R, :T]
            turned_real = (real * turn[:R] + imag * turn[R:]).astype(BF16)
            turned_imag = (imag * turn[:R] - real * turn[R:]).astype(BF16)
            rows[at : at + R, :T] = turned_real
            rows[at : at + R, T:] = turned_imag
            rows[at + R : at + 2 * R, :T] = turned_imag
            rows[at + R : at + 2 * R, T:] = -turned_real
        spectrum[g] = dot(inner[0], rows[...], 1, 1) + dot(inner[1], rows[...], 1, 1)

    def multiply(g):
        is_real = lax.broadcasted_iota(jnp.int32, (K, L), 1) < R
        for c in range(Q):
            lanes = slice(c * L, (c + 1) * L)
            response = filter_in[g, :, c].reshape(K, L).astype(F32)
            swapped = pltpu.roll(response, R, 1)
            value_c = spectrum[g, :, lanes]
            product[:, lanes] = (
                value_c * jnp.where(is_real, response, swapped)
                + pltpu.roll(value_c, R, 1) * jnp.where(is_real, -swapped, response)
            ).astype(BF16)

    def invert():
        back[...] = dot(product[...], inner[0], 0, 0) + dot(product[...], inner[1], 0, 0)

    def unturn():
        for c in range(Q):
            at = c * 2 * R
            real = back[at : at + R, :T] - back[at + R : at + 2 * R, T:]
            imag = back[at : at + R, T:] + back[at + R : at + 2 * R, :T]
            for at, part in (
                (at, real * turn[:R] - imag * turn[R:]),
                (at + R, real * turn[R:] + imag * turn[:R]),
            ):
                high, low = split(part)
                turned[at : at + R, :] = high
                turned[T + at : T + at + R, :] = high
                turned[2 * T + at : 2 * T + at + R, :] = low

    def finish(g):
        result = dot(last[...], turned[...], 1, 0)
        for c in range(Q):
            for i in range(T // L):
                staging[pl.ds(c * Q + i, S, stride=C), :] = result[
                    c * S : (c + 1) * S, i * L : (i + 1) * L
                ]
        conv_out[g] = staging[...].astype(BF16).reshape(S, C, L)

    def mix(g):
        staging[...] = conv_in[g].reshape(T, L).astype(F32)
        lanes = chunk_lanes(g)
        for i in range(T // L):
            tokens = slice(i * L, (i + 1) * L)
            convolved = staging[pl.ds(i, L, stride=Q), :].T
            gated = key[tokens, lanes].astype(F32) * value[tokens, lanes].astype(F32)
            mixed[tokens, lanes_at(level * T + g * L)] = (
                query[tokens, lanes].astype(F32) * (convolved + gain[:, lanes] * gated)
            ).astype(BF16)

    def project(source):
        return dot(mixed[:, share_lanes(source)], weight[source].reshape(T, T), 1, 0)

    def project_near():
        total = spectrum.at[0]
        total[...] = project(level)
        for k in (1, -1, 2, -2):
            total[...] += project(at_level(k))

    def project_next():
        total = spectrum.at[0]
        for k in (3, -3):
            total[...] += project(at_level(k))

    def project_last():
        out[...] = (spectrum[0] + project(at_level(4))).astype(BF16)

    def send_gated(g):
        send_all(gated_out.at[g], gated_in.at[g], sent_gated.at[g], got_gated.at[g])

    def send_filter(g):
        send_all(filter_out.at[g], filter_in.at[g], sent_filter.at[g], got_filter.at[g])

    def convolve(g):
        arrive(filter_in.at[g], got_filter.at[g])
        multiply(g)
        invert()
        unturn()
        finish(g)
        send_all(conv_out.at[g], conv_in.at[g], sent_conv.at[g], got_conv.at[g])

    def combine(g):
        arrive(conv_in.at[g], got_conv.at[g])
        mix(g)
        for part in range(2):
            for way in range(2):
                ring_send(way, 1, g, part)

    def begin(g):
        arrive(gated_in.at[g], got_gated.at[g])
        transform(g)

    def follow(g):
        send_gated(g)
        send_filter(g)

    for load in loads[:2]:
        load.wait()

    @pl.loop(0, G)
    def _(g):
        prepare_gated(g)

    for load in loads[2:4]:
        load.wait()
    prepare_filter()
    round_filter(0)
    pl.semaphore_wait(barrier, S + Z - 2)
    follow(0)
    round_filter(1)
    follow(1)
    for load in loads[4:]:
        load.wait()
    spread_share()
    round_filter(2)
    round_filter(3)

    begin(0)
    convolve(0)
    follow(2)
    begin(1)
    combine(0)
    convolve(1)
    follow(3)
    begin(2)
    forward(2, 0)
    combine(1)
    convolve(2)
    weight_first()
    forward(3, 0)
    begin(3)
    forward(2, 1)
    convolve(3)
    combine(2)
    forward(3, 1)
    weight_second()
    forward(4, 0)
    combine(3)
    forward(4, 1)
    forward(2, 2)
    forward(2, 3)
    forward(3, 2)
    weight_third()
    forward(3, 3)
    forward(4, 2)
    wait(weight.at[:, pl.ds(0, S // 2)], got_weight.at[4])
    project_near()
    forward(4, 3)
    project_next()
    for g in range(G):
        for way in range(2):
            ring_arrive(way, Z // 2, g, way)
    project_last()
    weight_sent()
    for g in range(G):
        arrive(gated_out.at[g], sent_gated.at[g])
        arrive(filter_out.at[g], sent_filter.at[g])
        arrive(conv_out.at[g], sent_conv.at[g])
        for hop in range(1, Z // 2 + 1):
            for way in range(2):
                for part in ring_parts(way, hop):
                    wait(ring_part(part, g, 0), sent_ring.at[way, hop - 1, g, part])


def body(gate_query, gate_key, gate_value, skip_gain, filter_spectra, out_weight):
    tab = tables()
    spectra = filter_spectra.reshape(KL * R, 2, G, L).transpose(0, 2, 1, 3)
    dma = pltpu.SemaphoreType.DMA
    return pl.pallas_call(
        kernel,
        out_shape=jax.ShapeDtypeStruct((T, T), BF16),
        in_specs=[pl.BlockSpec(memory_space=pltpu.HBM)] * (6 + len(NAMES)),
        out_specs=pl.BlockSpec(memory_space=VMEM),
        scratch_shapes=[
            VMEM((T, T), BF16),
            VMEM((T, T), BF16),
            VMEM((T, T), BF16),
            VMEM((1, T), F32),
            VMEM((KL * R * G * 2, L), BF16),
            VMEM((2 * R * G, 2 * R * G), BF16),
            VMEM((T, 2 * L), BF16),
            VMEM((2 * R, T), F32),
            VMEM((2, K, 2 * T), BF16),
            VMEM((L, 3 * T), BF16),
            VMEM((G, S, C, L), BF16),
            VMEM((G, S, C, L), BF16),
            VMEM((G, S, Q, KL, L), BF16),
            VMEM((G, S, Q, KL, L), BF16),
            VMEM((G, S, C, L), BF16),
            VMEM((G, S, C, L), BF16),
            VMEM((C, Z * T), BF16),
            VMEM((Z, S, C, T), BF16),
            VMEM((T, Z * T), BF16),
            VMEM((G, L * KL, L), F32),
            VMEM((T, 2 * T), BF16),
            VMEM((G, K, T), F32),
            VMEM((K, T), BF16),
            VMEM((T, 2 * T), F32),
            VMEM((3 * T, T), BF16),
            VMEM((T, L), F32),
            dma((11,)),
            dma((G,)),
            dma((G,)),
            dma((G,)),
            dma(()),
            dma((5,)),
            dma((2, Z // 2, G, 2)),
            dma((G,)),
            dma((G,)),
            dma((G,)),
            dma(()),
            dma((5,)),
            dma((2, Z // 2, G, 2)),
        ],
        compiler_params=pltpu.CompilerParams(
            collective_id=0, has_side_effects=True, vmem_limit_bytes=58 << 20
        ),
        cost_estimate=pl.CostEstimate(flops=12 * 10**9, bytes_accessed=8 << 20, transcendentals=0),
    )(
        gate_query,
        gate_key,
        gate_value,
        skip_gain[None, :],
        spectra.reshape(KL * R * G * 2, L),
        out_weight,
        *(jnp.asarray(tab[name]) for name in NAMES),
    )


def solution(mesh):
    placed = (
        P("seq", "ch"),
        P("seq", "ch"),
        P("seq", "ch"),
        P("ch"),
        P("seq", None, "ch"),
        P("ch", None),
    )
    return jax.shard_map(
        body, mesh=mesh, in_specs=placed, out_specs=P("seq", "ch"), check_vma=False
    )
```

```python
import functools

import jax
import jax.numpy as jnp
import ml_dtypes
import numpy as np
from jax import lax
from jax.experimental import pallas as pl
from jax.experimental.pallas import tpu as pltpu
from jax.sharding import PartitionSpec as P

S = 32
Z = 8
C = 16
Q = 4
G = C // Q
T = 512
R = 64
K = 512
L = 128
KL = K // S
N = R * K
AWAY = (
    (2, 2), (1, 2), (2, 1), (3, 2), (2, 3), (2, 0), (0, 2), (1, 1), (3, 3), (1, 3), (3, 1), (1, 0),
    (0, 1), (3, 0), (0, 3),
)
AWAY_X = sum(away[0] * 4**i for i, away in enumerate(AWAY))
AWAY_Y = sum(away[1] * 4**i for i, away in enumerate(AWAY))
MESH = pl.DeviceIdType.MESH
VMEM = pltpu.VMEM
BF16, F32 = jnp.bfloat16, jnp.float32


def halves(table):
    table = np.asarray(table, np.float64)
    high = table.astype(ml_dtypes.bfloat16)
    low = (table - high.astype(np.float64)).astype(ml_dtypes.bfloat16)
    return high, low


@functools.lru_cache(None)
def tables():
    p, s = np.arange(R), np.arange(S)
    tau, kappa = np.arange(T), np.arange(K)
    cross = 2 * np.pi * np.outer(p, s) / R
    each = np.eye(Q)
    first = np.concatenate([np.cos(cross), -np.sin(cross)], 0)
    first = np.concatenate(halves(np.kron(each, first)), 1)
    turn = 2 * np.pi * np.outer(p, tau) / N
    inner = 2 * np.pi * (np.outer(kappa, tau) % K) / K
    inner = np.concatenate([np.cos(inner), np.sin(inner)], 1)
    inner_high, inner_low = halves(inner)
    last = np.concatenate([np.cos(cross).T, -np.sin(cross).T], 1) / N
    last_high, last_low = halves(np.kron(each, last))
    last = np.concatenate([last_high, last_low, last_high], 1)
    order = np.zeros((2 * R * G, 2 * R * G), ml_dtypes.bfloat16)
    for q in range(R):
        for g in range(G):
            for part in range(2):
                order[(q * G + g) * 2 + part, (g * 2 + part) * R + q] = 1
    return dict(
        order=order,
        first=first,
        turn=np.concatenate([np.cos(turn), np.sin(turn)], 0).astype(np.float32),
        inner=np.stack([inner_high, inner_low]),
        last=last,
    )


NAMES = ("order", "first", "turn", "inner", "last")


def dot(left, right, left_dim, right_dim):
    return lax.dot_general(
        left, right, (((left_dim,), (right_dim,)), ((), ())), preferred_element_type=F32
    )


def split(values):
    high = values.astype(BF16)
    return high, (values - high.astype(F32)).astype(BF16)


def lanes_at(start, size=L):
    return pl.ds(start if isinstance(start, int) else pl.multiple_of(start, L), size)


def chunk_lanes(g):
    return lanes_at(g * L)


def kernel(
    query_here, key_here, value_here, gain_here, spectra_here, weight_here, order_here, first_here,
    turn_here, inner_here, last_here, out, query, key, value, gain, spectra, order, first, turn,
    inner, last, gated_out, gated_in, filter_out, filter_in, conv_out, conv_in, share, weight, mixed,
    wide, rows, spectrum, product, back, turned, staging, loaded, sent_gated, sent_filter, sent_conv,
    sent_share, sent_weight, sent_ring, got_gated, got_filter, got_conv, got_share, got_weight,
    got_ring,
):
    me, level = lax.axis_index("seq"), lax.axis_index("ch")
    core, x, y = lax.rem(me, 2), lax.rem(me // 2, 4), me // 8
    sibling = me + 1 - 2 * core

    def peer(k):
        away_x = lax.rem(k, 4)
        away_y = lax.rem(k // 4 + away_x, 4)
        return (
            lax.rem(y + away_y, 4) * 8 + lax.rem(x + away_x, 4) * 2 + lax.rem(core + k // 16, 2)
        )

    def at_level(k):
        return lax.rem(level + k + Z, Z)

    def along_x(k):
        return y * 8 + lax.rem(x + k, 4) * 2 + core

    def along_y(k):
        return lax.rem(y + k, 4) * 8 + x * 2 + core

    barrier = pltpu.get_barrier_semaphore()

    @pl.loop(1, S)
    def _(k):
        pl.semaphore_signal(barrier, inc=1, device_id={"seq": peer(k)}, device_id_type=MESH)

    @pl.loop(1, Z)
    def _(k):
        pl.semaphore_signal(barrier, inc=1, device_id={"ch": at_level(k)}, device_id_type=MESH)

    share_here = weight_here.at[pl.ds(pl.multiple_of(me * C, C), C), :]
    loads = [
        pltpu.make_async_copy(source, target, loaded.at[i])
        for i, (source, target) in enumerate(
            (
                (key_here, key), (value_here, value), (spectra_here, spectra), (order_here, order),
                (share_here, share), (first_here, first), (turn_here, turn), (inner_here, inner),
                (last_here, last), (query_here, query), (gain_here, gain),
            )
        )
    ]
    for load in loads:
        load.start()

    def send(source, target, sent, got, **to):
        pltpu.make_async_remote_copy(
            src_ref=source, dst_ref=target, send_sem=sent, recv_sem=got, device_id=to,
            device_id_type=MESH,
        ).start()

    def send_all(source, target, sent, got):
        def step(_, away):
            away_x, away_y = away
            chip = (
                lax.rem(y + lax.rem(away_y, 4), 4) * 8 + lax.rem(x + lax.rem(away_x, 4), 4) * 2
            )
            for c in range(2):
                send(source.at[chip + c], target.at[me], sent, got, seq=chip + c)
            return lax.div(away_x, 4), lax.div(away_y, 4)

        lax.fori_loop(0, len(AWAY), step, (jnp.int32(AWAY_X), jnp.int32(AWAY_Y)))
        send(source.at[sibling], target.at[me], sent, got, seq=sibling)
        target[me] = source[me]

    def wait(ref, sem):
        pltpu.make_async_copy(ref, ref, sem).wait()

    def arrive(target, sem):
        wait(target.at[pl.ds(0, S - 1)], sem)

    def share_lanes(k):
        return lanes_at(k * T, T)

    def spread_share():
        @pl.loop(1, Z)
        def _(k):
            to = at_level(k)
            send(
                share.at[:, share_lanes(to)], weight.at[level, me], sent_share, got_share, ch=to
            )

        weight[level, me] = share[:, share_lanes(level)]

    lower, upper = pl.ds(0, Z // 2), pl.ds(Z // 2, Z // 2)

    def weight_first():
        wait(weight.at[pl.ds(0, Z - 1), 0], got_share)

        @pl.loop(1, 4)
        def _(k):
            part = weight.at[lower, me]
            send(part, part, sent_weight.at[0], got_weight.at[0], seq=along_x(k))
            part = weight.at[upper, me]
            send(part, part, sent_weight.at[1], got_weight.at[1], seq=along_y(k))

    def weight_second():
        wait(weight.at[lower, pl.ds(0, 3)], got_weight.at[0])
        wait(weight.at[upper, pl.ds(0, 3)], got_weight.at[1])

        @pl.loop(1, 4)
        def _(k):
            @pl.loop(0, 4)
            def _(i):
                part = weight.at[lower, along_x(i)]
                send(part, part, sent_weight.at[2], got_weight.at[2], seq=along_y(k))
                part = weight.at[upper, along_y(i)]
                send(part, part, sent_weight.at[3], got_weight.at[3], seq=along_x(k))

    def weight_third():
        wait(weight.at[lower, pl.ds(0, 12)], got_weight.at[2])
        wait(weight.at[upper, pl.ds(0, 12)], got_weight.at[3])

        @pl.loop(0, S // 2)
        def _(i):
            part = weight.at[:, 2 * i + core]
            send(part, part, sent_weight.at[4], got_weight.at[4], seq=sibling)

    def weight_sent():
        wait(weight.at[pl.ds(0, Z - 1), 0], sent_share)
        wait(weight.at[lower, pl.ds(0, 3)], sent_weight.at[0])
        wait(weight.at[upper, pl.ds(0, 3)], sent_weight.at[1])
        wait(weight.at[lower, pl.ds(0, 12)], sent_weight.at[2])
        wait(weight.at[upper, pl.ds(0, 12)], sent_weight.at[3])
        wait(weight.at[:, pl.ds(0, S // 2)], sent_weight.at[4])

    def ring_parts(way, hop):
        return (way,) if hop == Z // 2 else (0, 1)

    def ring_part(part, g, source):
        return mixed.at[pl.ds(part * (T // 2), T // 2), lanes_at(source * T + g * L)]

    def ring_send(way, hop, g, part):
        sign = 1 - 2 * way
        piece = ring_part(part, g, at_level(-sign * (hop - 1)))
        send(
            piece, piece, sent_ring.at[way, hop - 1, g, part], got_ring.at[way, hop - 1, g, part],
            ch=at_level(sign),
        )

    def ring_arrive(way, hop, g, part):
        sign = 1 - 2 * way
        wait(ring_part(part, g, at_level(-sign * hop)), got_ring.at[way, hop - 1, g, part])

    def forward(hop, g):
        for part in range(2):
            for way in range(2):
                if part in ring_parts(way, hop - 1):
                    ring_arrive(way, hop - 1, g, part)
                if part in ring_parts(way, hop):
                    ring_send(way, hop, g, part)

    def prepare_gated(g):
        lanes = chunk_lanes(g)
        gated = (key[:, lanes].astype(F32) * value[:, lanes].astype(F32)).T
        for i in range(T // L):
            staging[pl.ds(i, L, stride=Q), :] = gated[:, i * L : (i + 1) * L]
        gated_out[g] = staging[...].astype(BF16).reshape(S, C, L)

    def prepare_filter():
        @pl.loop(0, KL)
        def _(k):
            block = spectra[pl.ds(pl.multiple_of(k * T, T), T), :]
            moved = dot(block, order[...], 0, 0)
            for g in range(G):
                wide[g, pl.ds(k, L, stride=KL), :] = moved[:, g * L : (g + 1) * L]

    def round_filter(g):
        filter_out[g] = wide[g].astype(BF16).reshape(S, Q, KL, L)

    def transform(g):
        staging[...] = gated_in[g].reshape(T, L).astype(F32)
        for c in range(Q):
            for i in range(T // L):
                part = staging[pl.ds(c * Q + i, S, stride=C), :].astype(BF16)
                for copy in range(2):
                    at = copy * L + c * S
                    turned[at : at + S, i * L : (i + 1) * L] = part
        back[:, :T] = dot(first[...], turned[: 2 * L, :], 1, 0)
        for c in range(Q):
            at = c * 2 * R
            real, imag = back[at : at + R, :T], back[at + R : at + 2 * R, :T]
            turned_real = (real * turn[:R] + imag * turn[R:]).astype(BF16)
            turned_imag = (imag * turn[:R] - real * turn[R:]).astype(BF16)
            rows[at : at + R, :T] = turned_real
            rows[at : at + R, T:] = turned_imag
            rows[at + R : at + 2 * R, :T] = turned_imag
            rows[at + R : at + 2 * R, T:] = -turned_real
        spectrum[g] = dot(inner[0], rows[...], 1, 1) + dot(inner[1], rows[...], 1, 1)

    def multiply(g):
        is_real = lax.broadcasted_iota(jnp.int32, (K, L), 1) < R
        for c in range(Q):
            lanes = slice(c * L, (c + 1) * L)
            response = filter_in[g, :, c].reshape(K, L).astype(F32)
            swapped = pltpu.roll(response, R, 1)
            value_c = spectrum[g, :, lanes]
            product[:, lanes] = (
                value_c * jnp.where(is_real, response, swapped)
                + pltpu.roll(value_c, R, 1) * jnp.where(is_real, -swapped, response)
            ).astype(BF16)

    def invert():
        back[...] = dot(product[...], inner[0], 0, 0) + dot(product[...], inner[1], 0, 0)

    def unturn():
        for c in range(Q):
            at = c * 2 * R
            real = back[at : at + R, :T] - back[at + R : at + 2 * R, T:]
            imag = back[at : at + R, T:] + back[at + R : at + 2 * R, :T]
            for at, part in (
                (at, real * turn[:R] - imag * turn[R:]),
                (at + R, real * turn[R:] + imag * turn[:R]),
            ):
                high, low = split(part)
                turned[at : at + R, :] = high
                turned[T + at : T + at + R, :] = high
                turned[2 * T + at : 2 * T + at + R, :] = low

    def finish(g):
        result = dot(last[...], turned[...], 1, 0)
        for c in range(Q):
            for i in range(T // L):
                staging[pl.ds(c * Q + i, S, stride=C), :] = result[
                    c * S : (c + 1) * S, i * L : (i + 1) * L
                ]
        conv_out[g] = staging[...].astype(BF16).reshape(S, C, L)

    def mix(g):
        staging[...] = conv_in[g].reshape(T, L).astype(F32)
        lanes = chunk_lanes(g)
        for i in range(T // L):
            tokens = slice(i * L, (i + 1) * L)
            convolved = staging[pl.ds(i, L, stride=Q), :].T
            gated = key[tokens, lanes].astype(F32) * value[tokens, lanes].astype(F32)
            mixed[tokens, lanes_at(level * T + g * L)] = (
                query[tokens, lanes].astype(F32) * (convolved + gain[:, lanes] * gated)
            ).astype(BF16)

    def project(source):
        return dot(mixed[:, share_lanes(source)], weight[source].reshape(T, T), 1, 0)

    def project_near():
        total = spectrum.at[0]
        total[...] = project(level)
        for k in (1, -1, 2, -2):
            total[...] += project(at_level(k))

    def project_next():
        total = spectrum.at[0]
        for k in (3, -3):
            total[...] += project(at_level(k))

    def project_last():
        out[...] = (spectrum[0] + project(at_level(4))).astype(BF16)

    def send_gated(g):
        send_all(gated_out.at[g], gated_in.at[g], sent_gated.at[g], got_gated.at[g])

    def send_filter(g):
        send_all(filter_out.at[g], filter_in.at[g], sent_filter.at[g], got_filter.at[g])

    def convolve(g):
        arrive(filter_in.at[g], got_filter.at[g])
        multiply(g)
        invert()
        unturn()
        finish(g)
        send_all(conv_out.at[g], conv_in.at[g], sent_conv.at[g], got_conv.at[g])

    def combine(g):
        arrive(conv_in.at[g], got_conv.at[g])
        mix(g)
        for part in range(2):
            for way in range(2):
                ring_send(way, 1, g, part)

    def begin(g):
        arrive(gated_in.at[g], got_gated.at[g])
        transform(g)

    def follow(g):
        send_gated(g)
        send_filter(g)

    for load in loads[:2]:
        load.wait()

    @pl.loop(0, G)
    def _(g):
        prepare_gated(g)

    for load in loads[2:4]:
        load.wait()
    prepare_filter()
    round_filter(0)
    pl.semaphore_wait(barrier, S + Z - 2)
    follow(0)
    round_filter(1)
    follow(1)
    for load in loads[4:]:
        load.wait()
    spread_share()
    round_filter(2)
    round_filter(3)

    begin(0)
    convolve(0)
    follow(2)
    begin(1)
    combine(0)
    convolve(1)
    follow(3)
    forward(2, 0)
    begin(2)
    combine(1)
    forward(3, 0)
    convolve(2)
    weight_first()
    begin(3)
    forward(2, 1)
    convolve(3)
    combine(2)
    forward(4, 0)
    forward(3, 1)
    weight_second()
    combine(3)
    forward(2, 2)
    forward(4, 1)
    forward(2, 3)
    forward(3, 2)
    weight_third()
    forward(3, 3)
    forward(4, 2)
    wait(weight.at[:, pl.ds(0, S // 2)], got_weight.at[4])
    project_near()
    forward(4, 3)
    project_next()
    for g in range(G):
        for way in range(2):
            ring_arrive(way, Z // 2, g, way)
    project_last()
    weight_sent()
    for g in range(G):
        arrive(gated_out.at[g], sent_gated.at[g])
        arrive(filter_out.at[g], sent_filter.at[g])
        arrive(conv_out.at[g], sent_conv.at[g])
        for hop in range(1, Z // 2 + 1):
            for way in range(2):
                for part in ring_parts(way, hop):
                    wait(ring_part(part, g, 0), sent_ring.at[way, hop - 1, g, part])


def body(gate_query, gate_key, gate_value, skip_gain, filter_spectra, out_weight):
    tab = tables()
    spectra = filter_spectra.reshape(KL * R, 2, G, L).transpose(0, 2, 1, 3)
    dma = pltpu.SemaphoreType.DMA
    return pl.pallas_call(
        kernel,
        out_shape=jax.ShapeDtypeStruct((T, T), BF16),
        in_specs=[pl.BlockSpec(memory_space=pltpu.HBM)] * (6 + len(NAMES)),
        out_specs=pl.BlockSpec(memory_space=VMEM),
        scratch_shapes=[
            VMEM((T, T), BF16),
            VMEM((T, T), BF16),
            VMEM((T, T), BF16),
            VMEM((1, T), F32),
            VMEM((KL * R * G * 2, L), BF16),
            VMEM((2 * R * G, 2 * R * G), BF16),
            VMEM((T, 2 * L), BF16),
            VMEM((2 * R, T), F32),
            VMEM((2, K, 2 * T), BF16),
            VMEM((L, 3 * T), BF16),
            VMEM((G, S, C, L), BF16),
            VMEM((G, S, C, L), BF16),
            VMEM((G, S, Q, KL, L), BF16),
            VMEM((G, S, Q, KL, L), BF16),
            VMEM((G, S, C, L), BF16),
            VMEM((G, S, C, L), BF16),
            VMEM((C, Z * T), BF16),
            VMEM((Z, S, C, T), BF16),
            VMEM((T, Z * T), BF16),
            VMEM((G, L * KL, L), F32),
            VMEM((T, 2 * T), BF16),
            VMEM((G, K, T), F32),
            VMEM((K, T), BF16),
            VMEM((T, 2 * T), F32),
            VMEM((3 * T, T), BF16),
            VMEM((T, L), F32),
            dma((11,)),
            dma((G,)),
            dma((G,)),
            dma((G,)),
            dma(()),
            dma((5,)),
            dma((2, Z // 2, G, 2)),
            dma((G,)),
            dma((G,)),
            dma((G,)),
            dma(()),
            dma((5,)),
            dma((2, Z // 2, G, 2)),
        ],
        compiler_params=pltpu.CompilerParams(
            collective_id=0, has_side_effects=True, vmem_limit_bytes=58 << 20
        ),
        cost_estimate=pl.CostEstimate(flops=12 * 10**9, bytes_accessed=8 << 20, transcendentals=0),
    )(
        gate_query,
        gate_key,
        gate_value,
        skip_gain[None, :],
        spectra.reshape(KL * R * G * 2, L),
        out_weight,
        *(jnp.asarray(tab[name]) for name in NAMES),
    )


def solution(mesh):
    placed = (
        P("seq", "ch"),
        P("seq", "ch"),
        P("seq", "ch"),
        P("ch"),
        P("seq", None, "ch"),
        P("ch", None),
    )
    return jax.shard_map(
        body, mesh=mesh, in_specs=placed, out_specs=P("seq", "ch"), check_vma=False
    )
```

```python
import functools

import jax
import jax.numpy as jnp
import ml_dtypes
import numpy as np
from jax import lax
from jax.experimental import pallas as pl
from jax.experimental.pallas import tpu as pltpu
from jax.sharding import PartitionSpec as P

S = 32
Z = 8
C = 16
Q = 4
G = C // Q
T = 512
R = 64
K = 512
L = 128
KL = K // S
N = R * K
MESH = pl.DeviceIdType.MESH
VMEM = pltpu.VMEM
BF16, F32 = jnp.bfloat16, jnp.float32


def halves(table):
    table = np.asarray(table, np.float64)
    high = table.astype(ml_dtypes.bfloat16)
    low = (table - high.astype(np.float64)).astype(ml_dtypes.bfloat16)
    return high, low


@functools.lru_cache(None)
def tables():
    p, s = np.arange(R), np.arange(S)
    tau, kappa = np.arange(T), np.arange(K)
    cross = 2 * np.pi * np.outer(p, s) / R
    each = np.eye(Q)
    first = np.concatenate([np.cos(cross), -np.sin(cross)], 0)
    first = np.concatenate(halves(np.kron(each, first)), 1)
    turn = 2 * np.pi * np.outer(p, tau) / N
    inner = 2 * np.pi * (np.outer(kappa, tau) % K) / K
    inner = np.concatenate([np.cos(inner), np.sin(inner)], 1)
    inner_high, inner_low = halves(inner)
    last = np.concatenate([np.cos(cross).T, -np.sin(cross).T], 1) / N
    last_high, last_low = halves(np.kron(each, last))
    last = np.concatenate([last_high, last_low, last_high], 1)
    order = np.zeros((2 * R * G, 2 * R * G), ml_dtypes.bfloat16)
    for q in range(R):
        for g in range(G):
            for part in range(2):
                order[(q * G + g) * 2 + part, (g * 2 + part) * R + q] = 1
    return dict(
        order=order,
        first=first,
        turn=np.concatenate([np.cos(turn), np.sin(turn)], 0).astype(np.float32),
        inner=np.stack([inner_high, inner_low]),
        last=last,
    )


NAMES = ("order", "first", "turn", "inner", "last")


def dot(left, right, left_dim, right_dim):
    return lax.dot_general(
        left, right, (((left_dim,), (right_dim,)), ((), ())), preferred_element_type=F32
    )


def split(values):
    high = values.astype(BF16)
    return high, (values - high.astype(F32)).astype(BF16)


def lanes_at(start, size=L):
    return pl.ds(start if isinstance(start, int) else pl.multiple_of(start, L), size)


def chunk_lanes(g):
    return lanes_at(g * L)


def kernel(
    query_here, key_here, value_here, gain_here, spectra_here, weight_here, order_here, first_here,
    turn_here, inner_here, last_here, out, query, key, value, gain, spectra, order, first, turn,
    inner, last, gated_out, gated_in, filter_out, filter_in, conv_out, conv_in, share, weight, mixed,
    wide, rows, spectrum, product, back, turned, staging, loaded, sent_gated, sent_filter, sent_conv,
    sent_share, sent_weight, sent_ring, got_gated, got_filter, got_conv, got_share, got_weight,
    got_ring,
):
    me, level = lax.axis_index("seq"), lax.axis_index("ch")
    core, x, y = lax.rem(me, 2), lax.rem(me // 2, 4), me // 8
    sibling = me + 1 - 2 * core

    def peer(k):
        away_x = lax.rem(k, 4)
        away_y = lax.rem(k // 4 + away_x, 4)
        return (
            lax.rem(y + away_y, 4) * 8 + lax.rem(x + away_x, 4) * 2 + lax.rem(core + k // 16, 2)
        )

    def at_level(k):
        return lax.rem(level + k + Z, Z)

    def along_x(k):
        return y * 8 + lax.rem(x + k, 4) * 2 + core

    def along_y(k):
        return lax.rem(y + k, 4) * 8 + x * 2 + core

    barrier = pltpu.get_barrier_semaphore()

    @pl.loop(1, S)
    def _(k):
        pl.semaphore_signal(barrier, inc=1, device_id={"seq": peer(k)}, device_id_type=MESH)

    @pl.loop(1, Z)
    def _(k):
        pl.semaphore_signal(barrier, inc=1, device_id={"ch": at_level(k)}, device_id_type=MESH)

    share_here = weight_here.at[pl.ds(pl.multiple_of(me * C, C), C), :]
    loads = [
        pltpu.make_async_copy(source, target, loaded.at[i])
        for i, (source, target) in enumerate(
            (
                (key_here, key), (value_here, value), (spectra_here, spectra), (order_here, order),
                (share_here, share), (first_here, first), (turn_here, turn), (inner_here, inner),
                (last_here, last), (query_here, query), (gain_here, gain),
            )
        )
    ]
    for load in loads:
        load.start()

    def send(source, target, sent, got, **to):
        pltpu.make_async_remote_copy(
            src_ref=source, dst_ref=target, send_sem=sent, recv_sem=got, device_id=to,
            device_id_type=MESH,
        ).start()

    def send_all(source, target, sent, got):
        @pl.loop(1, S)
        def _(k):
            send(source.at[peer(k)], target.at[me], sent, got, seq=peer(k))

        target[me] = source[me]

    def wait(ref, sem):
        pltpu.make_async_copy(ref, ref, sem).wait()

    def arrive(target, sem):
        wait(target.at[pl.ds(0, S - 1)], sem)

    def share_lanes(k):
        return lanes_at(k * T, T)

    def spread_share():
        @pl.loop(1, Z)
        def _(k):
            to = at_level(k)
            send(
                share.at[:, share_lanes(to)], weight.at[level, me], sent_share, got_share, ch=to
            )

        weight[level, me] = share[:, share_lanes(level)]

    lower, upper = pl.ds(0, Z // 2), pl.ds(Z // 2, Z // 2)

    def weight_first():
        wait(weight.at[pl.ds(0, Z - 1), 0], got_share)

        @pl.loop(1, 4)
        def _(k):
            part = weight.at[lower, me]
            send(part, part, sent_weight.at[0], got_weight.at[0], seq=along_x(k))
            part = weight.at[upper, me]
            send(part, part, sent_weight.at[1], got_weight.at[1], seq=along_y(k))

    def weight_second():
        wait(weight.at[lower, pl.ds(0, 3)], got_weight.at[0])
        wait(weight.at[upper, pl.ds(0, 3)], got_weight.at[1])

        @pl.loop(1, 4)
        def _(k):
            @pl.loop(0, 4)
            def _(i):
                part = weight.at[lower, along_x(i)]
                send(part, part, sent_weight.at[2], got_weight.at[2], seq=along_y(k))
                part = weight.at[upper, along_y(i)]
                send(part, part, sent_weight.at[3], got_weight.at[3], seq=along_x(k))

    def weight_third():
        wait(weight.at[lower, pl.ds(0, 12)], got_weight.at[2])
        wait(weight.at[upper, pl.ds(0, 12)], got_weight.at[3])

        @pl.loop(0, S // 2)
        def _(i):
            part = weight.at[:, 2 * i + core]
            send(part, part, sent_weight.at[4], got_weight.at[4], seq=sibling)

    def weight_sent():
        wait(weight.at[pl.ds(0, Z - 1), 0], sent_share)
        wait(weight.at[lower, pl.ds(0, 3)], sent_weight.at[0])
        wait(weight.at[upper, pl.ds(0, 3)], sent_weight.at[1])
        wait(weight.at[lower, pl.ds(0, 12)], sent_weight.at[2])
        wait(weight.at[upper, pl.ds(0, 12)], sent_weight.at[3])
        wait(weight.at[:, pl.ds(0, S // 2)], sent_weight.at[4])

    def ring_parts(way, hop):
        return (way,) if hop == Z // 2 else (0, 1)

    def ring_part(part, g, source):
        return mixed.at[pl.ds(part * (T // 2), T // 2), lanes_at(source * T + g * L)]

    def ring_send(way, hop, g, part):
        sign = 1 - 2 * way
        piece = ring_part(part, g, at_level(-sign * (hop - 1)))
        send(
            piece, piece, sent_ring.at[way, hop - 1, g, part], got_ring.at[way, hop - 1, g, part],
            ch=at_level(sign),
        )

    def ring_arrive(way, hop, g, part):
        sign = 1 - 2 * way
        wait(ring_part(part, g, at_level(-sign * hop)), got_ring.at[way, hop - 1, g, part])

    def forward(hop, g):
        for part in range(2):
            for way in range(2):
                if part in ring_parts(way, hop - 1):
                    ring_arrive(way, hop - 1, g, part)
                if part in ring_parts(way, hop):
                    ring_send(way, hop, g, part)

    def prepare_gated(g):
        lanes = chunk_lanes(g)
        gated = (key[:, lanes].astype(F32) * value[:, lanes].astype(F32)).T
        for i in range(T // L):
            staging[pl.ds(i, L, stride=Q), :] = gated[:, i * L : (i + 1) * L]
        gated_out[g] = staging[...].astype(BF16).reshape(S, C, L)

    def prepare_filter(g):
        @pl.loop(0, KL)
        def _(k):
            block = spectra[pl.ds(pl.multiple_of(k * T, T), T), :]
            wide[pl.ds(k, L, stride=KL), :] = dot(block, order[:, chunk_lanes(g)], 0, 0)

        filter_out[g] = wide[...].astype(BF16).reshape(S, Q, KL, L)

    def transform(g):
        staging[...] = gated_in[g].reshape(T, L).astype(F32)
        for c in range(Q):
            for i in range(T // L):
                part = staging[pl.ds(c * Q + i, S, stride=C), :].astype(BF16)
                for copy in range(2):
                    at = copy * L + c * S
                    turned[at : at + S, i * L : (i + 1) * L] = part
        back[:, :T] = dot(first[...], turned[: 2 * L, :], 1, 0)
        for c in range(Q):
            at = c * 2 * R
            real, imag = back[at : at + R, :T], back[at + R : at + 2 * R, :T]
            turned_real = (real * turn[:R] + imag * turn[R:]).astype(BF16)
            turned_imag = (imag * turn[:R] - real * turn[R:]).astype(BF16)
            rows[at : at + R, :T] = turned_real
            rows[at : at + R, T:] = turned_imag
            rows[at + R : at + 2 * R, :T] = turned_imag
            rows[at + R : at + 2 * R, T:] = -turned_real
        spectrum[g] = dot(inner[0], rows[...], 1, 1) + dot(inner[1], rows[...], 1, 1)

    def multiply(g):
        is_real = lax.broadcasted_iota(jnp.int32, (K, L), 1) < R
        for c in range(Q):
            lanes = slice(c * L, (c + 1) * L)
            response = filter_in[g, :, c].reshape(K, L).astype(F32)
            swapped = pltpu.roll(response, R, 1)
            value_c = spectrum[g, :, lanes]
            product[:, lanes] = (
                value_c * jnp.where(is_real, response, swapped)
                + pltpu.roll(value_c, R, 1) * jnp.where(is_real, -swapped, response)
            ).astype(BF16)

    def invert():
        back[...] = dot(product[...], inner[0], 0, 0) + dot(product[...], inner[1], 0, 0)

    def unturn():
        for c in range(Q):
            at = c * 2 * R
            real = back[at : at + R, :T] - back[at + R : at + 2 * R, T:]
            imag = back[at : at + R, T:] + back[at + R : at + 2 * R, :T]
            for at, part in (
                (at, real * turn[:R] - imag * turn[R:]),
                (at + R, real * turn[R:] + imag * turn[:R]),
            ):
                high, low = split(part)
                turned[at : at + R, :] = high
                turned[T + at : T + at + R, :] = high
                turned[2 * T + at : 2 * T + at + R, :] = low

    def finish(g):
        result = dot(last[...], turned[...], 1, 0)
        for c in range(Q):
            for i in range(T // L):
                staging[pl.ds(c * Q + i, S, stride=C), :] = result[
                    c * S : (c + 1) * S, i * L : (i + 1) * L
                ]
        conv_out[g] = staging[...].astype(BF16).reshape(S, C, L)

    def mix(g):
        staging[...] = conv_in[g].reshape(T, L).astype(F32)
        lanes = chunk_lanes(g)
        for i in range(T // L):
            tokens = slice(i * L, (i + 1) * L)
            convolved = staging[pl.ds(i, L, stride=Q), :].T
            gated = key[tokens, lanes].astype(F32) * value[tokens, lanes].astype(F32)
            mixed[tokens, lanes_at(level * T + g * L)] = (
                query[tokens, lanes].astype(F32) * (convolved + gain[:, lanes] * gated)
            ).astype(BF16)

    def project(source):
        return dot(mixed[:, share_lanes(source)], weight[source].reshape(T, T), 1, 0)

    def project_near():
        total = spectrum.at[0]
        total[...] = project(level)
        for k in (1, -1, 2, -2):
            total[...] += project(at_level(k))

    def project_next():
        total = spectrum.at[0]
        for k in (3, -3):
            total[...] += project(at_level(k))

    def project_last():
        out[...] = (spectrum[0] + project(at_level(4))).astype(BF16)

    def send_gated(g):
        send_all(gated_out.at[g], gated_in.at[g], sent_gated.at[g], got_gated.at[g])

    def send_filter(g):
        send_all(filter_out.at[g], filter_in.at[g], sent_filter.at[g], got_filter.at[g])

    def convolve(g):
        arrive(filter_in.at[g], got_filter.at[g])
        multiply(g)
        invert()
        unturn()
        finish(g)
        send_all(conv_out.at[g], conv_in.at[g], sent_conv.at[g], got_conv.at[g])

    def combine(g):
        arrive(conv_in.at[g], got_conv.at[g])
        mix(g)
        for part in range(2):
            for way in range(2):
                ring_send(way, 1, g, part)

    def begin(g):
        arrive(gated_in.at[g], got_gated.at[g])
        transform(g)

    def follow(g):
        send_gated(g)
        send_filter(g)

    for load in loads[:2]:
        load.wait()

    prepare_gated(0)
    for load in loads[2:4]:
        load.wait()
    prepare_filter(0)
    pl.semaphore_wait(barrier, S + Z - 2)
    follow(0)
    prepare_gated(1)
    prepare_filter(1)
    follow(1)
    for load in loads[4:]:
        load.wait()
    spread_share()

    @pl.loop(2, G)
    def _(g):
        prepare_gated(g)
        prepare_filter(g)

    begin(0)
    convolve(0)
    follow(2)
    begin(1)
    combine(0)
    convolve(1)
    follow(3)
    begin(2)
    forward(2, 0)
    combine(1)
    convolve(2)
    weight_first()
    forward(3, 0)
    begin(3)
    forward(2, 1)
    convolve(3)
    combine(2)
    forward(3, 1)
    weight_second()
    forward(4, 0)
    combine(3)
    forward(4, 1)
    forward(2, 2)
    forward(2, 3)
    forward(3, 2)
    weight_third()
    forward(3, 3)
    forward(4, 2)
    wait(weight.at[:, pl.ds(0, S // 2)], got_weight.at[4])
    project_near()
    forward(4, 3)
    project_next()
    for g in range(G):
        for way in range(2):
            ring_arrive(way, Z // 2, g, way)
    project_last()
    weight_sent()
    for g in range(G):
        arrive(gated_out.at[g], sent_gated.at[g])
        arrive(filter_out.at[g], sent_filter.at[g])
        arrive(conv_out.at[g], sent_conv.at[g])
        for hop in range(1, Z // 2 + 1):
            for way in range(2):
                for part in ring_parts(way, hop):
                    wait(ring_part(part, g, 0), sent_ring.at[way, hop - 1, g, part])


def body(gate_query, gate_key, gate_value, skip_gain, filter_spectra, out_weight):
    tab = tables()
    spectra = filter_spectra.reshape(KL * R, 2, G, L).transpose(0, 2, 1, 3)
    dma = pltpu.SemaphoreType.DMA
    return pl.pallas_call(
        kernel,
        out_shape=jax.ShapeDtypeStruct((T, T), BF16),
        in_specs=[pl.BlockSpec(memory_space=pltpu.HBM)] * (6 + len(NAMES)),
        out_specs=pl.BlockSpec(memory_space=VMEM),
        scratch_shapes=[
            VMEM((T, T), BF16),
            VMEM((T, T), BF16),
            VMEM((T, T), BF16),
            VMEM((1, T), F32),
            VMEM((KL * R * G * 2, L), BF16),
            VMEM((2 * R * G, 2 * R * G), BF16),
            VMEM((T, 2 * L), BF16),
            VMEM((2 * R, T), F32),
            VMEM((2, K, 2 * T), BF16),
            VMEM((L, 3 * T), BF16),
            VMEM((G, S, C, L), BF16),
            VMEM((G, S, C, L), BF16),
            VMEM((G, S, Q, KL, L), BF16),
            VMEM((G, S, Q, KL, L), BF16),
            VMEM((G, S, C, L), BF16),
            VMEM((G, S, C, L), BF16),
            VMEM((C, Z * T), BF16),
            VMEM((Z, S, C, T), BF16),
            VMEM((T, Z * T), BF16),
            VMEM((L * KL, L), F32),
            VMEM((T, 2 * T), BF16),
            VMEM((G, K, T), F32),
            VMEM((K, T), BF16),
            VMEM((T, 2 * T), F32),
            VMEM((3 * T, T), BF16),
            VMEM((T, L), F32),
            dma((11,)),
            dma((G,)),
            dma((G,)),
            dma((G,)),
            dma(()),
            dma((5,)),
            dma((2, Z // 2, G, 2)),
            dma((G,)),
            dma((G,)),
            dma((G,)),
            dma(()),
            dma((5,)),
            dma((2, Z // 2, G, 2)),
        ],
        compiler_params=pltpu.CompilerParams(
            collective_id=0, has_side_effects=True, vmem_limit_bytes=58 << 20
        ),
        cost_estimate=pl.CostEstimate(flops=12 * 10**9, bytes_accessed=8 << 20, transcendentals=0),
    )(
        gate_query,
        gate_key,
        gate_value,
        skip_gain[None, :],
        spectra.reshape(KL * R * G * 2, L),
        out_weight,
        *(jnp.asarray(tab[name]) for name in NAMES),
    )


def solution(mesh):
    placed = (
        P("seq", "ch"),
        P("seq", "ch"),
        P("seq", "ch"),
        P("ch"),
        P("seq", None, "ch"),
        P("ch", None),
    )
    return jax.shard_map(
        body, mesh=mesh, in_specs=placed, out_specs=P("seq", "ch"), check_vma=False
    )
```

```python
import functools

import jax
import jax.numpy as jnp
import ml_dtypes
import numpy as np
from jax import lax
from jax.experimental import pallas as pl
from jax.experimental.pallas import tpu as pltpu
from jax.sharding import PartitionSpec as P

S = 32
Z = 8
C = 16
Q = 4
G = C // Q
T = 512
R = 64
K = 512
L = 128
KL = K // S
N = R * K
MESH = pl.DeviceIdType.MESH
VMEM = pltpu.VMEM
BF16, F32 = jnp.bfloat16, jnp.float32


def halves(table):
    table = np.asarray(table, np.float64)
    high = table.astype(ml_dtypes.bfloat16)
    low = (table - high.astype(np.float64)).astype(ml_dtypes.bfloat16)
    return high, low


@functools.lru_cache(None)
def tables():
    p, s = np.arange(R), np.arange(S)
    tau, kappa = np.arange(T), np.arange(K)
    cross = 2 * np.pi * np.outer(p, s) / R
    each = np.eye(Q)
    first = np.concatenate([np.cos(cross), -np.sin(cross)], 0)
    first = np.concatenate(halves(np.kron(each, first)), 1)
    turn = 2 * np.pi * np.outer(p, tau) / N
    inner = 2 * np.pi * (np.outer(kappa, tau) % K) / K
    inner = np.concatenate([np.cos(inner), np.sin(inner)], 1)
    inner_high, inner_low = halves(inner)
    last = np.concatenate([np.cos(cross).T, -np.sin(cross).T], 1) / N
    last_high, last_low = halves(np.kron(each, last))
    last = np.concatenate([last_high, last_low, last_high], 1)
    order = np.zeros((2 * R * G, 2 * R * G), ml_dtypes.bfloat16)
    for q in range(R):
        for g in range(G):
            for part in range(2):
                order[(q * G + g) * 2 + part, (g * 2 + part) * R + q] = 1
    return dict(
        order=order,
        first=first,
        turn=np.concatenate([np.cos(turn), np.sin(turn)], 0).astype(np.float32),
        inner=np.stack([inner_high, inner_low]),
        last=last,
    )


NAMES = ("order", "first", "turn", "inner", "last")


def dot(left, right, left_dim, right_dim):
    return lax.dot_general(
        left, right, (((left_dim,), (right_dim,)), ((), ())), preferred_element_type=F32
    )


def split(values):
    high = values.astype(BF16)
    return high, (values - high.astype(F32)).astype(BF16)


def lanes_at(start, size=L):
    return pl.ds(start if isinstance(start, int) else pl.multiple_of(start, L), size)


def chunk_lanes(g):
    return lanes_at(g * L)


def kernel(
    query_here, key_here, value_here, gain_here, spectra_here, weight_here, order_here, first_here,
    turn_here, inner_here, last_here, out, query, key, value, gain, spectra, order, first, turn,
    inner, last, gated_out, gated_in, filter_out, filter_in, conv_out, conv_in, share, weight, mixed,
    wide, rows, spectrum, product, back, turned, staging, loaded, sent_gated, sent_filter, sent_conv,
    sent_share, sent_weight, sent_ring, got_gated, got_filter, got_conv, got_share, got_weight,
    got_ring,
):
    me, level = lax.axis_index("seq"), lax.axis_index("ch")
    core, x, y = lax.rem(me, 2), lax.rem(me // 2, 4), me // 8
    sibling = me + 1 - 2 * core

    def peer(k):
        away_x = lax.rem(k, 4)
        away_y = lax.rem(k // 4 + away_x, 4)
        return (
            lax.rem(y + away_y, 4) * 8 + lax.rem(x + away_x, 4) * 2 + lax.rem(core + k // 16, 2)
        )

    def at_level(k):
        return lax.rem(level + k + Z, Z)

    def along_x(k):
        return y * 8 + lax.rem(x + k, 4) * 2 + core

    def along_y(k):
        return lax.rem(y + k, 4) * 8 + x * 2 + core

    barrier = pltpu.get_barrier_semaphore()

    @pl.loop(1, S)
    def _(k):
        pl.semaphore_signal(barrier, inc=1, device_id={"seq": peer(k)}, device_id_type=MESH)

    @pl.loop(1, Z)
    def _(k):
        pl.semaphore_signal(barrier, inc=1, device_id={"ch": at_level(k)}, device_id_type=MESH)

    share_here = weight_here.at[pl.ds(pl.multiple_of(me * C, C), C), :]
    loads = [
        pltpu.make_async_copy(source, target, loaded.at[i])
        for i, (source, target) in enumerate(
            (
                (key_here, key), (value_here, value), (spectra_here, spectra), (order_here, order),
                (share_here, share), (first_here, first), (turn_here, turn), (inner_here, inner),
                (last_here, last), (query_here, query), (gain_here, gain),
            )
        )
    ]
    for load in loads:
        load.start()

    def send(source, target, sent, got, **to):
        pltpu.make_async_remote_copy(
            src_ref=source, dst_ref=target, send_sem=sent, recv_sem=got, device_id=to,
            device_id_type=MESH,
        ).start()

    def send_all(source, target, sent, got):
        @pl.loop(1, S)
        def _(k):
            send(source.at[peer(k)], target.at[me], sent, got, seq=peer(k))

        target[me] = source[me]

    def wait(ref, sem):
        pltpu.make_async_copy(ref, ref, sem).wait()

    def arrive(target, sem):
        wait(target.at[pl.ds(0, S - 1)], sem)

    def share_lanes(k):
        return lanes_at(k * T, T)

    def spread_share():
        @pl.loop(1, Z)
        def _(k):
            to = at_level(k)
            send(
                share.at[:, share_lanes(to)], weight.at[level, me], sent_share, got_share, ch=to
            )

        weight[level, me] = share[:, share_lanes(level)]

    lower, upper = pl.ds(0, Z // 2), pl.ds(Z // 2, Z // 2)

    def weight_first():
        wait(weight.at[pl.ds(0, Z - 1), 0], got_share)

        @pl.loop(1, 4)
        def _(k):
            part = weight.at[lower, me]
            send(part, part, sent_weight.at[0], got_weight.at[0], seq=along_x(k))
            part = weight.at[upper, me]
            send(part, part, sent_weight.at[1], got_weight.at[1], seq=along_y(k))

    def weight_second():
        wait(weight.at[lower, pl.ds(0, 3)], got_weight.at[0])
        wait(weight.at[upper, pl.ds(0, 3)], got_weight.at[1])

        @pl.loop(1, 4)
        def _(k):
            @pl.loop(0, 4)
            def _(i):
                part = weight.at[lower, along_x(i)]
                send(part, part, sent_weight.at[2], got_weight.at[2], seq=along_y(k))
                part = weight.at[upper, along_y(i)]
                send(part, part, sent_weight.at[3], got_weight.at[3], seq=along_x(k))

    def weight_third():
        wait(weight.at[lower, pl.ds(0, 12)], got_weight.at[2])
        wait(weight.at[upper, pl.ds(0, 12)], got_weight.at[3])

        @pl.loop(0, S // 2)
        def _(i):
            part = weight.at[:, 2 * i + core]
            send(part, part, sent_weight.at[4], got_weight.at[4], seq=sibling)

    def weight_sent():
        wait(weight.at[pl.ds(0, Z - 1), 0], sent_share)
        wait(weight.at[lower, pl.ds(0, 3)], sent_weight.at[0])
        wait(weight.at[upper, pl.ds(0, 3)], sent_weight.at[1])
        wait(weight.at[lower, pl.ds(0, 12)], sent_weight.at[2])
        wait(weight.at[upper, pl.ds(0, 12)], sent_weight.at[3])
        wait(weight.at[:, pl.ds(0, S // 2)], sent_weight.at[4])

    def ring_parts(way, hop):
        return (way,) if hop == Z // 2 else (0, 1)

    def ring_part(part, g, source):
        return mixed.at[pl.ds(part * (T // 2), T // 2), lanes_at(source * T + g * L)]

    def ring_send(way, hop, g, part):
        sign = 1 - 2 * way
        piece = ring_part(part, g, at_level(-sign * (hop - 1)))
        send(
            piece, piece, sent_ring.at[way, hop - 1, g, part], got_ring.at[way, hop - 1, g, part],
            ch=at_level(sign),
        )

    def ring_arrive(way, hop, g, part):
        sign = 1 - 2 * way
        wait(ring_part(part, g, at_level(-sign * hop)), got_ring.at[way, hop - 1, g, part])

    def forward(hop, g):
        for part in range(2):
            for way in range(2):
                if part in ring_parts(way, hop - 1):
                    ring_arrive(way, hop - 1, g, part)
                if part in ring_parts(way, hop):
                    ring_send(way, hop, g, part)

    def prepare_gated(g):
        lanes = chunk_lanes(g)
        gated = (key[:, lanes].astype(F32) * value[:, lanes].astype(F32)).T
        for i in range(T // L):
            staging[pl.ds(i, L, stride=Q), :] = gated[:, i * L : (i + 1) * L]
        gated_out[g] = staging[...].astype(BF16).reshape(S, C, L)

    def prepare_filter():
        @pl.loop(0, KL)
        def _(k):
            block = spectra[pl.ds(pl.multiple_of(k * T, T), T), :]
            moved = dot(block, order[...], 0, 0)
            for g in range(G):
                wide[g, pl.ds(k, L, stride=KL), :] = moved[:, g * L : (g + 1) * L]

    def round_filter(g):
        filter_out[g] = wide[g].astype(BF16).reshape(S, Q, KL, L)

    def transform(g):
        staging[...] = gated_in[g].reshape(T, L).astype(F32)
        for c in range(Q):
            for i in range(T // L):
                part = staging[pl.ds(c * Q + i, S, stride=C), :].astype(BF16)
                for copy in range(2):
                    at = copy * L + c * S
                    turned[at : at + S, i * L : (i + 1) * L] = part
        back[:, :T] = dot(first[...], turned[: 2 * L, :], 1, 0)
        for c in range(Q):
            at = c * 2 * R
            real, imag = back[at : at + R, :T], back[at + R : at + 2 * R, :T]
            turned_real = (real * turn[:R] + imag * turn[R:]).astype(BF16)
            turned_imag = (imag * turn[:R] - real * turn[R:]).astype(BF16)
            rows[at : at + R, :T] = turned_real
            rows[at : at + R, T:] = turned_imag
            rows[at + R : at + 2 * R, :T] = turned_imag
            rows[at + R : at + 2 * R, T:] = -turned_real
        spectrum[g] = dot(inner[0], rows[...], 1, 1) + dot(inner[1], rows[...], 1, 1)

    def multiply(g):
        is_real = lax.broadcasted_iota(jnp.int32, (K, L), 1) < R
        for c in range(Q):
            lanes = slice(c * L, (c + 1) * L)
            response = filter_in[g, :, c].reshape(K, L).astype(F32)
            swapped = pltpu.roll(response, R, 1)
            value_c = spectrum[g, :, lanes]
            product[:, lanes] = (
                value_c * jnp.where(is_real, response, swapped)
                + pltpu.roll(value_c, R, 1) * jnp.where(is_real, -swapped, response)
            ).astype(BF16)

    def invert():
        back[...] = dot(product[...], inner[0], 0, 0) + dot(product[...], inner[1], 0, 0)

    def unturn():
        for c in range(Q):
            at = c * 2 * R
            real = back[at : at + R, :T] - back[at + R : at + 2 * R, T:]
            imag = back[at : at + R, T:] + back[at + R : at + 2 * R, :T]
            for at, part in (
                (at, real * turn[:R] - imag * turn[R:]),
                (at + R, real * turn[R:] + imag * turn[:R]),
            ):
                high, low = split(part)
                turned[at : at + R, :] = high
                turned[T + at : T + at + R, :] = high
                turned[2 * T + at : 2 * T + at + R, :] = low

    def finish(g):
        result = dot(last[...], turned[...], 1, 0)
        for c in range(Q):
            for i in range(T // L):
                staging[pl.ds(c * Q + i, S, stride=C), :] = result[
                    c * S : (c + 1) * S, i * L : (i + 1) * L
                ]
        conv_out[g] = staging[...].astype(BF16).reshape(S, C, L)

    def mix(g):
        staging[...] = conv_in[g].reshape(T, L).astype(F32)
        lanes = chunk_lanes(g)
        for i in range(T // L):
            tokens = slice(i * L, (i + 1) * L)
            convolved = staging[pl.ds(i, L, stride=Q), :].T
            gated = key[tokens, lanes].astype(F32) * value[tokens, lanes].astype(F32)
            mixed[tokens, lanes_at(level * T + g * L)] = (
                query[tokens, lanes].astype(F32) * (convolved + gain[:, lanes] * gated)
            ).astype(BF16)

    def project(source):
        return dot(mixed[:, share_lanes(source)], weight[source].reshape(T, T), 1, 0)

    def project_near():
        total = spectrum.at[0]
        total[...] = project(level)
        for k in (1, -1, 2, -2):
            total[...] += project(at_level(k))

    def project_next():
        total = spectrum.at[0]
        for k in (3, -3):
            total[...] += project(at_level(k))

    def project_last():
        out[...] = (spectrum[0] + project(at_level(4))).astype(BF16)

    def send_gated(g):
        send_all(gated_out.at[g], gated_in.at[g], sent_gated.at[g], got_gated.at[g])

    def send_filter(g):
        send_all(filter_out.at[g], filter_in.at[g], sent_filter.at[g], got_filter.at[g])

    def convolve(g):
        arrive(filter_in.at[g], got_filter.at[g])
        multiply(g)
        invert()
        unturn()
        finish(g)
        send_all(conv_out.at[g], conv_in.at[g], sent_conv.at[g], got_conv.at[g])

    def combine(g):
        arrive(conv_in.at[g], got_conv.at[g])
        mix(g)
        for part in range(2):
            for way in range(2):
                ring_send(way, 1, g, part)

    def begin(g):
        arrive(gated_in.at[g], got_gated.at[g])
        transform(g)

    def follow(g):
        send_gated(g)
        send_filter(g)

    for load in loads[:2]:
        load.wait()

    @pl.loop(0, G)
    def _(g):
        prepare_gated(g)

    for load in loads[2:4]:
        load.wait()
    prepare_filter()
    round_filter(0)
    pl.semaphore_wait(barrier, S + Z - 2)
    follow(0)
    round_filter(1)
    follow(1)
    for load in loads[4:]:
        load.wait()
    spread_share()
    round_filter(2)
    round_filter(3)

    begin(0)
    convolve(0)
    follow(2)
    begin(1)
    combine(0)
    convolve(1)
    follow(3)
    forward(2, 0)
    begin(2)
    combine(1)
    forward(3, 0)
    convolve(2)
    weight_first()
    begin(3)
    forward(2, 1)
    convolve(3)
    combine(2)
    forward(4, 0)
    forward(3, 1)
    weight_second()
    combine(3)
    forward(2, 2)
    forward(4, 1)
    forward(2, 3)
    forward(3, 2)
    weight_third()
    forward(3, 3)
    forward(4, 2)
    wait(weight.at[:, pl.ds(0, S // 2)], got_weight.at[4])
    project_near()
    forward(4, 3)
    project_next()
    for g in range(G):
        for way in range(2):
            ring_arrive(way, Z // 2, g, way)
    project_last()
    weight_sent()
    for g in range(G):
        arrive(gated_out.at[g], sent_gated.at[g])
        arrive(filter_out.at[g], sent_filter.at[g])
        arrive(conv_out.at[g], sent_conv.at[g])
        for hop in range(1, Z // 2 + 1):
            for way in range(2):
                for part in ring_parts(way, hop):
                    wait(ring_part(part, g, 0), sent_ring.at[way, hop - 1, g, part])


def body(gate_query, gate_key, gate_value, skip_gain, filter_spectra, out_weight):
    tab = tables()
    spectra = filter_spectra.reshape(KL * R, 2, G, L).transpose(0, 2, 1, 3)
    dma = pltpu.SemaphoreType.DMA
    return pl.pallas_call(
        kernel,
        out_shape=jax.ShapeDtypeStruct((T, T), BF16),
        in_specs=[pl.BlockSpec(memory_space=pltpu.HBM)] * (6 + len(NAMES)),
        out_specs=pl.BlockSpec(memory_space=VMEM),
        scratch_shapes=[
            VMEM((T, T), BF16),
            VMEM((T, T), BF16),
            VMEM((T, T), BF16),
            VMEM((1, T), F32),
            VMEM((KL * R * G * 2, L), BF16),
            VMEM((2 * R * G, 2 * R * G), BF16),
            VMEM((T, 2 * L), BF16),
            VMEM((2 * R, T), F32),
            VMEM((2, K, 2 * T), BF16),
            VMEM((L, 3 * T), BF16),
            VMEM((G, S, C, L), BF16),
            VMEM((G, S, C, L), BF16),
            VMEM((G, S, Q, KL, L), BF16),
            VMEM((G, S, Q, KL, L), BF16),
            VMEM((G, S, C, L), BF16),
            VMEM((G, S, C, L), BF16),
            VMEM((C, Z * T), BF16),
            VMEM((Z, S, C, T), BF16),
            VMEM((T, Z * T), BF16),
            VMEM((G, L * KL, L), F32),
            VMEM((T, 2 * T), BF16),
            VMEM((G, K, T), F32),
            VMEM((K, T), BF16),
            VMEM((T, 2 * T), F32),
            VMEM((3 * T, T), BF16),
            VMEM((T, L), F32),
            dma((11,)),
            dma((G,)),
            dma((G,)),
            dma((G,)),
            dma(()),
            dma((5,)),
            dma((2, Z // 2, G, 2)),
            dma((G,)),
            dma((G,)),
            dma((G,)),
            dma(()),
            dma((5,)),
            dma((2, Z // 2, G, 2)),
        ],
        compiler_params=pltpu.CompilerParams(
            collective_id=0, has_side_effects=True, vmem_limit_bytes=58 << 20
        ),
        cost_estimate=pl.CostEstimate(flops=12 * 10**9, bytes_accessed=8 << 20, transcendentals=0),
    )(
        gate_query,
        gate_key,
        gate_value,
        skip_gain[None, :],
        spectra.reshape(KL * R * G * 2, L),
        out_weight,
        *(jnp.asarray(tab[name]) for name in NAMES),
    )


def solution(mesh):
    placed = (
        P("seq", "ch"),
        P("seq", "ch"),
        P("seq", "ch"),
        P("ch"),
        P("seq", None, "ch"),
        P("ch", None),
    )
    return jax.shard_map(
        body, mesh=mesh, in_specs=placed, out_specs=P("seq", "ch"), check_vma=False
    )
```
